32 devices in a mesh: groups: 2 (over x), leaf: 16 (over z, y, core).
Axes of the slice: x: 2, y: 2, z: 4, core: 2. Of those that a mesh axis runs over, the one named last changes fastest.
Arguments:
- right_side: float32 [65536, 256], P(('groups', 'leaf')), parts along dimension 0, may hold values from -6 to 6
- cotangent: float32 [65536, 256], P(('groups', 'leaf')), parts along dimension 0, may hold values from -6 to 6
- coeff_basis: float32 [4, 64, 65536], P(None, None, ('groups', 'leaf')), parts along dimension 2, may hold values from -1 to 1
- saved_basis: float32 [4, 64, 65536], P(None, None, ('groups', 'leaf')), parts along dimension 2, may hold values from -0.24 to 0.24
- node_inverse: float32 [30, 128, 128], P('groups'), parts along dimension 0, may hold values from -1 to 2.5
- leaf_rows: int32 [32], P(('groups', 'leaf')), parts along dimension 0, may hold values from 1 to 2048, 24576 in all
Outputs:
- solution: float32 [65536, 256], P(('groups', 'leaf')), parts along dimension 0
- grad_left: bfloat16 [4, 64, 65536], P(None, None, ('groups', 'leaf')), parts along dimension 2
- grad_right: bfloat16 [4, 64, 65536], P(None, None, ('groups', 'leaf')), parts along dimension 2
The draws below stay inside these ranges and needn't reach their ends.
There are 2 independent parts, one for each index of `groups`. The reference program is written for one: setup_inputs(seed, part) draws one part's arguments, and reference() takes and returns one part's arrays. A program takes and returns all parts, laid end to end along the dimension named above; each array names one. Nothing has to cross between parts.
Inputs may be any that keep to these rules, and one draw needn't show every extreme that they name: `leaf_rows`: every leaf has at least one live row; the live rows of all leaves sum to 24576, and some leaf has all 2048 rows live.
All inputs are finite; a program needn't handle non-finite values. No bound on the sum of `leaf_rows` on one device may be relied on, other than what follows from the above.
Results may differ from the reference program's by a relative error of at most 0.001.
Values sent between devices are 32-bit elements; how exact they have to be, the bound alone decides.
No kernel may reach another device: no remote copies, remote signals or barrier semaphores. Data moves between devices by JAX's collectives and lax.ppermute only.
A program may use at most 64 MiB of HBM per device.

```python
import math
import jax
import jax.numpy as jnp
import numpy as np
from jax import lax

RANK = 64
COLS = 256
ROWS_DEV = 2048
LEVELS = 4
NODES = 15
SIDE0 = 1
N_ROWS = 32768
N_LEAF = 16


def draw_coeff_basis(key, part):
    level_scale = 1.0 / jnp.sqrt(ROWS_DEV * SIDE0 * 2.0 ** jnp.arange(LEVELS, dtype=jnp.float32))
    sample = jnp.clip(jax.random.normal(key, (LEVELS, RANK, N_ROWS), jnp.float32), -4.0, 4.0)
    return sample * level_scale[:, None, None]


def draw_node_inverse(key, part):
    order_two = 2 * RANK
    identity = jnp.eye(order_two, dtype=jnp.float32)
    first_key = jax.random.fold_in(key, 11)
    spread_part = jnp.clip(jax.random.normal(first_key, (NODES, order_two, order_two), jnp.float32), -4.0, 4.0)
    diag_gain = jnp.ones((NODES, order_two), jnp.float32)
    return identity[None] * diag_gain[:, :, None] + spread_part * (0.5 / jnp.sqrt(jnp.float32(order_two)))


def levels(stream_key, shape, pieces, smallest, top_value):
    factor_of = 1.0
    for dim, parts in pieces:
        heights = jax.random.uniform(jax.random.fold_in(jax.random.fold_in(stream_key, 6), dim), (parts,), jnp.float32, smallest / len(pieces), top_value / len(pieces))
        factor_of = factor_of * jnp.repeat(jnp.exp(heights), shape[dim] // parts).reshape((-1,) + (1,) * (len(shape) - 1 - dim))
    return factor_of


def length_profile(number_of, total, bound, slope):
    loads = [(1 << 20) // math.isqrt(grade ** slope) + 1 for grade in range(2, number_of + 1)]
    surplus, holding = total - bound - (number_of - 1), [1] * (number_of - 1)
    while surplus > 0:
        free = [i for i in range(number_of - 1) if holding[i] < bound]
        whole, budget = sum([loads[i] for i in free]), surplus
        for i in free:
            extra = min(bound - holding[i], max(1, budget * loads[i] // whole), surplus)
            holding[i] = holding[i] + extra
            surplus = surplus - extra
    return np.array([bound] + holding)


def uneven_parts(stream_key, amount, total, bound, skew):
    if amount == 2:
        one = jax.random.randint(stream_key, (), max(1, total - bound), min(bound, total - 1) + 1)
        return jnp.stack([one, total - one])
    sizes = jnp.asarray(length_profile(amount, total, bound, skew), jnp.int32)
    pairs = (amount - 1) // 2
    donor, sink = sizes[1:1 + 2 * pairs:2], sizes[2:2 + 2 * pairs:2]
    slack = jnp.minimum(donor - 1, bound - sink)
    shifted = jax.random.randint(jax.random.fold_in(stream_key, 1), (pairs,), 0, 1 << 20) % (slack + 1)
    sizes = sizes.at[1:1 + 2 * pairs:2].set(donor - shifted).at[2:2 + 2 * pairs:2].set(sink + shifted)
    return sizes[jax.random.permutation(jax.random.fold_in(stream_key, 2), amount)]


def normal_values(key, shape, scale, bound, pieces=(), kind=jnp.bfloat16):
    entries = jax.random.normal(key, shape, jnp.float32) * scale
    if len(pieces) > 0:
        entries = levels(key, shape, pieces, -0.22, 0.18) * entries
    return jnp.clip(entries, min=-bound, max=bound).astype(kind)


def setup_inputs(seed: int = 0, part: int = 0) -> dict:
    streams_of = jax.random.split(jax.random.key(seed), 7)
    own_keys = jax.random.split(jax.random.fold_in(streams_of[6], part), 7)
    right_side = normal_values(own_keys[0], (N_ROWS, COLS), 1.0, 6.0, ((0, 16),), jnp.float32)
    cotangent = normal_values(own_keys[1], (N_ROWS, COLS), 1.0, 6.0, ((0, 16),), jnp.float32)
    coeff_basis = draw_coeff_basis(jax.random.fold_in(jax.random.fold_in(streams_of[6], part), 71), part)
    saved_basis = normal_values(own_keys[3], (LEVELS, RANK, N_ROWS), 0.04, 0.24, ((2, 16),), jnp.float32)
    node_inverse = draw_node_inverse(jax.random.fold_in(jax.random.fold_in(streams_of[6], part), 71), part)
    leaf_rows = uneven_parts(own_keys[5], N_LEAF, N_LEAF * ROWS_DEV * 3 // 4, ROWS_DEV, 1).astype(jnp.int32)
    return {"right_side": right_side, "cotangent": cotangent, "coeff_basis": coeff_basis, "saved_basis": saved_basis, "node_inverse": node_inverse, "leaf_rows": leaf_rows}


def reference(right_side, cotangent, coeff_basis, saved_basis, node_inverse, leaf_rows):
    highest = lax.Precision.HIGHEST
    row_count = right_side.shape[0]
    within = jnp.arange(row_count, dtype=jnp.int32) % ROWS_DEV
    live_rows = (within < jnp.repeat(leaf_rows, ROWS_DEV)).astype(jnp.float32)
    current = right_side * live_rows[:, None]
    weights = cotangent * live_rows[:, None]
    saved_masked = saved_basis * live_rows[None, None, :]
    for height in range(LEVELS):
        side_count = 2 ** (LEVELS - height)
        side_rows = row_count // side_count
        basis_now = coeff_basis[height].reshape(RANK, side_count, side_rows)
        blocks = current.reshape(side_count, side_rows, COLS)
        coeffs = jnp.einsum('rsi,sic->src', basis_now, blocks, precision=highest)
        paired = coeffs.reshape(side_count // 2, 2 * RANK, COLS)
        offset = 2 ** LEVELS - side_count
        inverse = node_inverse[offset:offset + side_count // 2]
        mixture = jnp.einsum('nab,nbc->nac', inverse, paired, precision=highest).reshape(side_count, RANK, COLS)
        correction = jnp.einsum('rsi,src->sic', saved_masked[height].reshape(RANK, side_count, side_rows), mixture, precision=highest)
        current = current - correction.reshape(row_count, COLS)
    scale_factor = 1.0 / jnp.sqrt(jnp.float32(COLS))
    left_list = []
    right_list = []
    for height in range(LEVELS):
        side_count = 2 ** (LEVELS - height)
        side_rows = row_count // side_count
        basis_now = coeff_basis[height].reshape(RANK, side_count, side_rows)
        wblocks = weights.reshape(side_count, side_rows, COLS)
        fblocks = current.reshape(side_count, side_rows, COLS)
        k_sums = jnp.einsum('rsi,sic->src', basis_now, wblocks, precision=highest)
        l_sums = jnp.einsum('rsi,sic->src', basis_now, fblocks, precision=highest)
        k_swap = k_sums.reshape(side_count // 2, 2, RANK, COLS)[:, ::-1].reshape(side_count, RANK, COLS)
        l_swap = l_sums.reshape(side_count // 2, 2, RANK, COLS)[:, ::-1].reshape(side_count, RANK, COLS)
        left_now = jnp.einsum('src,sic->rsi', l_swap, wblocks, precision=highest) * scale_factor
        right_now = jnp.einsum('src,sic->rsi', k_swap, fblocks, precision=highest) * scale_factor
        left_list.append(left_now.reshape(RANK, row_count))
        right_list.append(right_now.reshape(RANK, row_count))
    grad_left = jnp.stack(left_list).astype(jnp.bfloat16)
    grad_right = jnp.stack(right_list).astype(jnp.bfloat16)
    return (current, grad_left, grad_right)
```

```python
import functools

import jax
import jax.numpy as jnp
from jax import lax
from jax.experimental import pallas as pl
from jax.experimental.pallas import tpu as pltpu
from jax.sharding import PartitionSpec as P


HIGH = lax.Precision.HIGH
F32 = jnp.float32


def dot(a, b, dims=((1,), (0,))):
    return lax.dot_general(a, b, (dims, ((), ())), precision=HIGH, preferred_element_type=F32)


def pack(blocks):
    rows = []
    for i in range(0, len(blocks) - 1, 2):
        rows.append(jnp.concatenate([blocks[i], blocks[i + 1]], 1))
    if len(blocks) % 2:
        half = blocks[-1].shape[0] // 2
        rows.append(jnp.concatenate([blocks[-1][:half], blocks[-1][half:]], 1))
    return rows


def pack_rows(count, rank):
    return count // 2 * rank + count % 2 * (rank // 2)


def unpack(ref, start, count, rank):
    blocks = []
    for i in range(count):
        if i == count - 1 and count % 2:
            half = ref[start : start + rank // 2, :]
            blocks.append(jnp.concatenate([half[:, :rank], half[:, rank:]], 0))
        else:
            lane = i % 2 * rank
            blocks.append(ref[start : start + rank, lane : lane + rank])
            start += i % 2 * rank
    return blocks


def solve_rows(level, levels, rank):
    return rank + pack_rows(levels - 1 - level, rank)


def side_rows(level, levels, rank):
    return rank + pack_rows(levels - level, rank)


def local_kernel(dims, rows_ref, x_ref, w_ref, u_ref, q_ref, node_ref, *refs):
    levels, rank, base_bits, chunk = dims
    solve_keep, solve_send, side_keep, side_send, nodes_out, c_acc, k_acc, g_acc, sems = refs
    step = pl.program_id(0)
    position = lax.axis_index("leaf")

    def node_copy(k):
        index = 2**levels - 2 ** (levels - k) + jnp.right_shift(position, base_bits + k + 1)
        return pltpu.make_async_copy(node_ref.at[index], nodes_out.at[k], sems.at[k])

    @pl.when(step == 0)
    def _():
        for k in range(levels):
            node_copy(k).start()
        c_acc[...] = jnp.zeros_like(c_acc)
        k_acc[...] = jnp.zeros_like(k_acc)
        g_acc[...] = jnp.zeros_like(g_acc)

    place = step * chunk + lax.broadcasted_iota(jnp.int32, (1, chunk), 1)
    u = jnp.where(place < rows_ref[0], u_ref[...], 0.0)
    c_acc[...] += dot(u, x_ref[...])
    k_acc[...] += dot(u, w_ref[...])
    g_acc[...] += dot(u, q_ref[...], ((1,), (1,)))

    @pl.when(step == pl.num_programs(0) - 1)
    def _():
        half = c_acc.shape[1] // 2
        is_first = position % 2 == 0

        def block(i, j):
            return g_acc[i * rank : (i + 1) * rank, j * rank : (j + 1) * rank]

        def write(keep, send, acc, blocks_of):
            at = 0
            for k in range(levels):
                low = acc[k * rank : (k + 1) * rank, :half]
                high = acc[k * rank : (k + 1) * rank, half:]
                keep[at : at + rank, :] = jnp.where(is_first, low, high)
                send[at : at + rank, :] = jnp.where(is_first, high, low)
                at += rank
                for rows in pack(blocks_of(k)):
                    keep[at : at + rows.shape[0], :] = rows
                    send[at : at + rows.shape[0], :] = rows
                    at += rows.shape[0]

        write(solve_keep, solve_send, c_acc, lambda k: [block(i, k) for i in range(k + 1, levels)])
        write(side_keep, side_send, k_acc, lambda k: [block(k, j) for j in range(k, levels)])
        for k in range(levels):
            node_copy(k).wait()


def level_kernel(dims, level, own_ref, sib_ref, nodes_ref, z_ref, *next_ref):
    levels, rank, base_bits = dims
    is_lower = jnp.right_shift(lax.axis_index("leaf"), base_bits + level) % 2 == 0
    own, sib = own_ref[:rank, :], sib_ref[:rank, :]
    both = jnp.concatenate([jnp.where(is_lower, own, sib), jnp.where(is_lower, sib, own)], 0)
    mixed = dot(nodes_ref[level], both)
    z_own = jnp.where(is_lower, mixed[:rank], mixed[rank:])
    z_sib = jnp.where(is_lower, mixed[rank:], mixed[:rank])
    z_ref[:rank, :] = z_own
    z_ref[rank:, :] = z_sib
    if not next_ref:
        return
    (out_ref,) = next_ref
    count = levels - 1 - level
    h_own = unpack(own_ref, rank, count, rank)
    h_sib = unpack(sib_ref, rank, count, rank)
    h_both = jnp.concatenate(
        [jnp.concatenate(h_own, 0), jnp.concatenate(h_sib, 0)], 1
    )
    drop = dot(h_both, jnp.concatenate([z_own, z_sib], 0))
    start = solve_rows(level, levels, rank)
    at = 0
    for i in range(count):
        out_ref[at : at + rank, :] = (
            own_ref[start + at : start + at + rank, :]
            + sib_ref[start + at : start + at + rank, :]
            - drop[i * rank : (i + 1) * rank]
        )
        at += rank
        rest = solve_rows(level + 1 + i, levels, rank) - rank
        if rest:
            out_ref[at : at + rest, :] = (
                own_ref[start + at : start + at + rest, :] + sib_ref[start + at : start + at + rest, :]
            )
            at += rest


def end_kernel(dims, scale, pair, *refs):
    levels, rank = dims
    sib_solve, sib_side, z_refs = refs[:levels], refs[levels : 2 * levels], refs[2 * levels : 3 * levels]
    refs = refs[3 * levels :]
    z_all = jnp.concatenate([z_ref[:rank, :] for z_ref in z_refs], 0)

    def lower_term(k, solve_ref, side_ref, z_here):
        blocks = unpack(side_ref, rank, levels - k, rank)
        if k + 1 < levels:
            z_here = jnp.concatenate([z_here, z_all[(k + 1) * rank :]], 0)
        return (solve_ref[:rank, :] - dot(jnp.concatenate(blocks, 1), z_here)) * scale

    def write(out_ref, k, z_term, l_term, k_term):
        for part, term in enumerate((z_term, l_term, k_term)):
            at = (part * levels + k) * rank
            out_ref[at : at + rank, :] = term

    for k in range(levels):
        z_own, z_sib = z_refs[k][:rank, :], z_refs[k][rank:, :]
        terms = (z_own, lower_term(k, sib_solve[k], sib_side[k], z_sib), sib_side[k][:rank, :] * scale)
        write(refs[-1], k, *terms)
        if pair:
            own_solve, own_side, send_ref = refs[:3]
            if k == 0:
                terms = (z_sib, lower_term(0, own_solve, own_side, z_own), own_side[:rank, :] * scale)
            write(send_ref, k, *terms)


def final_kernel(chunk, rows_ref, own_ref, other_ref, x_ref, w_ref, q_ref, sol_ref, left_ref, right_ref):
    is_first = lax.axis_index("leaf") % 2 == 0
    count = own_ref.shape[0] // 3

    def whole(part):
        own = own_ref[part * count : (part + 1) * count, :]
        other = other_ref[part * count : (part + 1) * count, :]
        return jnp.concatenate([jnp.where(is_first, own, other), jnp.where(is_first, other, own)], 1)

    first = pl.program_id(0) * chunk
    live_row = first + lax.broadcasted_iota(jnp.int32, (chunk, 1), 0) < rows_ref[0]
    live_lane = first + lax.broadcasted_iota(jnp.int32, (1, chunk), 1) < rows_ref[0]
    x = x_ref[...] - dot(q_ref[...], whole(0), ((0,), (0,)))
    x = jnp.where(live_row, x, 0.0)
    sol_ref[...] = x
    left = dot(whole(1), w_ref[...], ((1,), (1,)))
    left_ref[...] = jnp.where(live_lane, left, 0.0).astype(left_ref.dtype)
    right_ref[...] = dot(whole(2), x, ((1,), (1,))).astype(right_ref.dtype)


def swapped(value, bit):
    mask = 2**bit
    pairs = [(source, source ^ mask) for source in range(lax.axis_size("leaf"))]
    return lax.ppermute(value, "leaf", pairs)


def body(right_side, cotangent, coeff_basis, saved_basis, node_inverse, leaf_rows):
    row_count, col_count = right_side.shape
    levels, rank = coeff_basis.shape[:2]
    wide = levels * rank
    half = col_count // 2
    base_bits = lax.axis_size("leaf").bit_length() - 1 - levels
    chunk = min(512, row_count)
    steps = row_count // chunk
    u_all = coeff_basis.reshape(wide, row_count)
    q_all = saved_basis.reshape(wide, row_count)

    smem = pl.BlockSpec(memory_space=pltpu.SMEM)
    by_row = pl.BlockSpec((chunk, col_count), lambda i: (i, 0))
    by_lane = pl.BlockSpec((wide, chunk), lambda i: (0, i))

    def fixed(*shape):
        return pl.BlockSpec(shape, lambda i: (0,) * len(shape))

    n_solve = sum(solve_rows(k, levels, rank) for k in range(levels))
    n_side = sum(side_rows(k, levels, rank) for k in range(levels))
    order = 2 * rank
    shapes = [(n_solve, half)] * 2 + [(n_side, half)] * 2 + [(levels, order, order)]
    solve, solve_send, side, side_send, nodes = pl.pallas_call(
        functools.partial(local_kernel, (levels, rank, base_bits, chunk)),
        grid=(steps,),
        out_shape=[jax.ShapeDtypeStruct(s, F32) for s in shapes],
        in_specs=[smem, by_row, by_row, by_lane, by_lane, pl.BlockSpec(memory_space=pl.ANY)],
        out_specs=[fixed(*s) for s in shapes],
        scratch_shapes=[pltpu.VMEM((wide, col_count), F32)] * 2
        + [pltpu.VMEM((wide, wide), F32), pltpu.SemaphoreType.DMA((levels,))],
        name="local_sums",
    )(leaf_rows, right_side, cotangent, u_all, q_all, node_inverse)

    if base_bits == 0:
        sib_solve, sib_side = swapped(solve_send, 0), swapped(side_send, 0)
    else:
        solve, side = solve + swapped(solve_send, 0), side + swapped(side_send, 0)
        for bit in range(1, base_bits):
            solve, side = solve + swapped(solve, bit), side + swapped(side, bit)
        sib_solve, sib_side = swapped(solve, base_bits), swapped(side, base_bits)

    vmem = pl.BlockSpec(memory_space=pltpu.VMEM)
    first_solve, first_side = solve, side
    solves, sides, zs = [], [], []
    for k in range(levels):
        if k > 0:
            sib_solve, sib_side = swapped(solve, base_bits + k), swapped(side, base_bits + k)
        solves.append(sib_solve)
        sides.append(sib_side)
        rows = solve.shape[0] - solve_rows(k, levels, rank)
        out_shape = [jax.ShapeDtypeStruct((order, half), F32)]
        if rows:
            out_shape.append(jax.ShapeDtypeStruct((rows, half), F32))
        outs = pl.pallas_call(
            functools.partial(level_kernel, (levels, rank, base_bits), k),
            out_shape=out_shape,
            in_specs=[vmem] * 3,
            out_specs=[vmem] * len(out_shape),
            name=f"level_{k}",
        )(solve, sib_solve, nodes)
        zs.append(outs[0])
        if rows:
            solve = outs[1]
            side = (side + sib_side)[side_rows(k, levels, rank) :]

    pair = base_bits == 0
    ends = [*solves, *sides, *zs] + ([first_solve, first_side] if pair else [])
    *send, own = pl.pallas_call(
        functools.partial(end_kernel, (levels, rank), 1.0 / col_count**0.5, pair),
        out_shape=[jax.ShapeDtypeStruct((3 * wide, half), F32)] * (2 if pair else 1),
        in_specs=[vmem] * len(ends),
        out_specs=[vmem] * (2 if pair else 1),
        name="end_factors",
    )(*ends)
    other = swapped(send[0] if pair else own, 0)

    sol, left, right = pl.pallas_call(
        functools.partial(final_kernel, chunk),
        grid=(steps,),
        out_shape=[
            jax.ShapeDtypeStruct((row_count, col_count), F32),
            jax.ShapeDtypeStruct((wide, row_count), jnp.bfloat16),
            jax.ShapeDtypeStruct((wide, row_count), jnp.bfloat16),
        ],
        in_specs=[smem, fixed(3 * wide, half), fixed(3 * wide, half), by_row, by_row, by_lane],
        out_specs=[by_row, by_lane, by_lane],
        name="row_outputs",
    )(leaf_rows, own, other, right_side, cotangent, q_all)
    return sol, left.reshape(coeff_basis.shape), right.reshape(coeff_basis.shape)


def solution(mesh):
    in_specs = (
        P(("groups", "leaf"), None),
        P(("groups", "leaf"), None),
        P(None, None, ("groups", "leaf")),
        P(None, None, ("groups", "leaf")),
        P("groups", None, None),
        P(("groups", "leaf")),
    )
    out_specs = (
        P(("groups", "leaf"), None),
        P(None, None, ("groups", "leaf")),
        P(None, None, ("groups", "leaf")),
    )
    return jax.shard_map(body, mesh=mesh, in_specs=in_specs, out_specs=out_specs, check_vma=False)
```

```python
import functools

import jax
import jax.numpy as jnp
from jax import lax
from jax.experimental import pallas as pl
from jax.experimental.pallas import tpu as pltpu
from jax.sharding import PartitionSpec as P


HIGH = lax.Precision.HIGH
F32 = jnp.float32
MIB = 2**20


def dot(a, b, dims=((1,), (0,))):
    return lax.dot_general(a, b, (dims, ((), ())), precision=HIGH, preferred_element_type=F32)


def pack(blocks):
    rows = []
    for i in range(0, len(blocks) - 1, 2):
        rows.append(jnp.concatenate([blocks[i], blocks[i + 1]], 1))
    if len(blocks) % 2:
        half = blocks[-1].shape[0] // 2
        rows.append(jnp.concatenate([blocks[-1][:half], blocks[-1][half:]], 1))
    return rows


def pack_rows(count, rank):
    return count // 2 * rank + count % 2 * (rank // 2)


def unpack(ref, start, count, rank):
    blocks = []
    for i in range(count):
        if i == count - 1 and count % 2:
            half = ref[start : start + rank // 2, :]
            blocks.append(jnp.concatenate([half[:, :rank], half[:, rank:]], 0))
        else:
            lane = i % 2 * rank
            blocks.append(ref[start : start + rank, lane : lane + rank])
            start += i % 2 * rank
    return blocks


def solve_rows(level, levels, rank):
    return rank + pack_rows(levels - 1 - level, rank)


def side_rows(level, levels, rank):
    return rank + pack_rows(levels - level, rank)


def masked(rows_ref, u_ref, chunk):
    place = pl.program_id(0) * chunk + lax.broadcasted_iota(jnp.int32, (1, chunk), 1)
    return jnp.where(place < rows_ref[0], u_ref[...], 0.0)


def write_state(keep, send, acc, rank, blocks_of):
    half = acc.shape[1] // 2
    is_first = lax.axis_index("leaf") % 2 == 0
    at = 0
    for k in range(acc.shape[0] // rank):
        low = acc[k * rank : (k + 1) * rank, :half]
        high = acc[k * rank : (k + 1) * rank, half:]
        keep[at : at + rank, :] = jnp.where(is_first, low, high)
        send[at : at + rank, :] = jnp.where(is_first, high, low)
        at += rank
        for rows in pack(blocks_of(k)):
            keep[at : at + rows.shape[0], :] = rows
            send[at : at + rows.shape[0], :] = rows
            at += rows.shape[0]


def local_kernel(dims, rows_ref, x_ref, u_ref, q_ref, node_ref, keep, send, g_ref, nodes_out, c_acc, sems):
    levels, rank, base_bits, chunk = dims
    step = pl.program_id(0)

    def node_copy(k):
        position = lax.axis_index("leaf")
        index = 2**levels - 2 ** (levels - k) + jnp.right_shift(position, base_bits + k + 1)
        return pltpu.make_async_copy(node_ref.at[index], nodes_out.at[k], sems.at[k])

    @pl.when(step == 0)
    def _():
        for k in range(levels):
            node_copy(k).start()
        c_acc[...] = jnp.zeros_like(c_acc)
        g_ref[...] = jnp.zeros_like(g_ref)

    u = masked(rows_ref, u_ref, chunk)
    c_acc[...] += dot(u, x_ref[...])
    g_ref[...] += dot(u, q_ref[...], ((1,), (1,)))

    @pl.when(step == pl.num_programs(0) - 1)
    def _():
        def blocks(k):
            lane = slice(k * rank, (k + 1) * rank)
            return [g_ref[i * rank : (i + 1) * rank, lane] for i in range(k + 1, levels)]

        write_state(keep, send, c_acc, rank, blocks)
        for k in range(levels):
            node_copy(k).wait()


def side_kernel(dims, rows_ref, w_ref, u_ref, g_ref, keep, send, k_acc):
    levels, rank, chunk = dims
    step = pl.program_id(0)

    @pl.when(step == 0)
    def _():
        k_acc[...] = jnp.zeros_like(k_acc)

    k_acc[...] += dot(masked(rows_ref, u_ref, chunk), w_ref[...])

    @pl.when(step == pl.num_programs(0) - 1)
    def _():
        def blocks(k):
            row = slice(k * rank, (k + 1) * rank)
            return [g_ref[row, j * rank : (j + 1) * rank] for j in range(k, levels)]

        write_state(keep, send, k_acc, rank, blocks)


def side_sum_kernel(start, own_ref, sib_ref, after_ref, out_ref):
    del after_ref
    out_ref[...] = own_ref[start:, :] + sib_ref[start:, :]


def level_kernel(dims, level, own_ref, sib_ref, nodes_ref, z_ref, *next_ref):
    levels, rank, base_bits = dims
    is_lower = jnp.right_shift(lax.axis_index("leaf"), base_bits + level) % 2 == 0
    own, sib = own_ref[:rank, :], sib_ref[:rank, :]
    both = jnp.concatenate([jnp.where(is_lower, own, sib), jnp.where(is_lower, sib, own)], 0)
    mixed = dot(nodes_ref[level], both)
    z_own = jnp.where(is_lower, mixed[:rank], mixed[rank:])
    z_sib = jnp.where(is_lower, mixed[rank:], mixed[:rank])
    z_ref[:rank, :] = z_own
    z_ref[rank:, :] = z_sib
    if not next_ref:
        return
    (out_ref,) = next_ref
    count = levels - 1 - level
    h_own = unpack(own_ref, rank, count, rank)
    h_sib = unpack(sib_ref, rank, count, rank)
    h_both = jnp.concatenate(
        [jnp.concatenate(h_own, 0), jnp.concatenate(h_sib, 0)], 1
    )
    drop = dot(h_both, jnp.concatenate([z_own, z_sib], 0))
    start = solve_rows(level, levels, rank)
    at = 0
    for i in range(count):
        out_ref[at : at + rank, :] = (
            own_ref[start + at : start + at + rank, :]
            + sib_ref[start + at : start + at + rank, :]
            - drop[i * rank : (i + 1) * rank]
        )
        at += rank
        rest = solve_rows(level + 1 + i, levels, rank) - rank
        if rest:
            out_ref[at : at + rest, :] = (
                own_ref[start + at : start + at + rest, :] + sib_ref[start + at : start + at + rest, :]
            )
            at += rest


def end_kernel(dims, scale, pair, *refs):
    levels, rank = dims
    sib_solve, sib_side, z_refs = refs[:levels], refs[levels : 2 * levels], refs[2 * levels : 3 * levels]
    refs = refs[3 * levels :]
    z_all = jnp.concatenate([z_ref[:rank, :] for z_ref in z_refs], 0)

    def lower_term(k, solve_ref, side_ref, z_here):
        blocks = unpack(side_ref, rank, levels - k, rank)
        if k + 1 < levels:
            z_here = jnp.concatenate([z_here, z_all[(k + 1) * rank :]], 0)
        return (solve_ref[:rank, :] - dot(jnp.concatenate(blocks, 1), z_here)) * scale

    def write(out_ref, k, z_term, l_term, k_term):
        for part, term in enumerate((z_term, l_term, k_term)):
            at = (part * levels + k) * rank
            out_ref[at : at + rank, :] = term

    for k in range(levels):
        z_own, z_sib = z_refs[k][:rank, :], z_refs[k][rank:, :]
        terms = (z_own, lower_term(k, sib_solve[k], sib_side[k], z_sib), sib_side[k][:rank, :] * scale)
        write(refs[-1], k, *terms)
        if pair:
            own_solve, own_side, send_ref = refs[:3]
            if k == 0:
                terms = (z_sib, lower_term(0, own_solve, own_side, z_own), own_side[:rank, :] * scale)
            write(send_ref, k, *terms)


def final_kernel(chunk, rows_ref, own_ref, other_ref, x_ref, w_ref, q_ref, sol_ref, left_ref, right_ref):
    is_first = lax.axis_index("leaf") % 2 == 0
    count = own_ref.shape[0] // 3

    def whole(part):
        own = own_ref[part * count : (part + 1) * count, :]
        other = other_ref[part * count : (part + 1) * count, :]
        return jnp.concatenate([jnp.where(is_first, own, other), jnp.where(is_first, other, own)], 1)

    first = pl.program_id(0) * chunk
    live_row = first + lax.broadcasted_iota(jnp.int32, (chunk, 1), 0) < rows_ref[0]
    live_lane = first + lax.broadcasted_iota(jnp.int32, (1, chunk), 1) < rows_ref[0]
    x = x_ref[...] - dot(q_ref[...], whole(0), ((0,), (0,)))
    x = jnp.where(live_row, x, 0.0)
    sol_ref[...] = x
    left = dot(whole(1), w_ref[...], ((1,), (1,)))
    left_ref[...] = jnp.where(live_lane, left, 0.0).astype(left_ref.dtype)
    right_ref[...] = dot(whole(2), x, ((1,), (1,))).astype(right_ref.dtype)


def swapped(value, bit):
    mask = 2**bit
    pairs = [(source, source ^ mask) for source in range(lax.axis_size("leaf"))]
    return lax.ppermute(value, "leaf", pairs)


def body(right_side, cotangent, coeff_basis, saved_basis, node_inverse, leaf_rows):
    row_count, col_count = right_side.shape
    levels, rank = coeff_basis.shape[:2]
    wide = levels * rank
    half = col_count // 2
    base_bits = lax.axis_size("leaf").bit_length() - 1 - levels
    chunk = min(512, row_count)
    steps = row_count // chunk
    u_all = coeff_basis.reshape(wide, row_count)
    q_all = saved_basis.reshape(wide, row_count)

    smem = pl.BlockSpec(memory_space=pltpu.SMEM)
    by_row = pl.BlockSpec((chunk, col_count), lambda i: (i, 0))
    by_lane = pl.BlockSpec((wide, chunk), lambda i: (0, i))

    def fixed(*shape):
        return pl.BlockSpec(shape, lambda i: (0,) * len(shape))

    n_solve = sum(solve_rows(k, levels, rank) for k in range(levels))
    n_side = sum(side_rows(k, levels, rank) for k in range(levels))
    order = 2 * rank
    params = pltpu.CompilerParams(vmem_limit_bytes=24 * MIB)
    hbm = [pltpu.with_memory_space_constraint(a, pltpu.HBM) for a in (right_side, u_all, q_all, node_inverse)]
    shapes = [(n_solve, half)] * 2 + [(wide, wide), (levels, order, order)]
    solve, solve_send, products, nodes = pl.pallas_call(
        functools.partial(local_kernel, (levels, rank, base_bits, chunk)),
        grid=(steps,),
        out_shape=[jax.ShapeDtypeStruct(s, F32) for s in shapes],
        in_specs=[smem, by_row, by_lane, by_lane, pl.BlockSpec(memory_space=pl.ANY)],
        out_specs=[fixed(*s) for s in shapes],
        scratch_shapes=[pltpu.VMEM((wide, col_count), F32), pltpu.SemaphoreType.DMA((levels,))],
        compiler_params=params,
        name="local_sums",
    )(leaf_rows, *hbm)
    side, side_send = pl.pallas_call(
        functools.partial(side_kernel, (levels, rank, chunk)),
        grid=(steps,),
        out_shape=[jax.ShapeDtypeStruct((n_side, half), F32)] * 2,
        in_specs=[smem, by_row, by_lane, fixed(wide, wide)],
        out_specs=[fixed(n_side, half)] * 2,
        scratch_shapes=[pltpu.VMEM((wide, col_count), F32)],
        compiler_params=params,
        cost_estimate=pl.CostEstimate(
            flops=6 * wide * row_count * col_count, bytes_accessed=8 * wide * row_count, transcendentals=0
        ),
        name="side_sums",
    )(leaf_rows, cotangent, u_all, products)

    if base_bits == 0:
        sib_solve, sib_side = swapped(solve_send, 0), swapped(side_send, 0)
    else:
        solve, side = solve + swapped(solve_send, 0), side + swapped(side_send, 0)
        for bit in range(1, base_bits):
            solve, side = solve + swapped(solve, bit), side + swapped(side, bit)
        sib_solve, sib_side = swapped(solve, base_bits), swapped(side, base_bits)

    vmem = pl.BlockSpec(memory_space=pltpu.VMEM)
    small = pltpu.CompilerParams(vmem_limit_bytes=4 * MIB)
    first_solve, first_side = solve, side
    solves, sides, zs = [], [], []
    for k in range(levels):
        if k > 0:
            sib_solve, sib_side = swapped(solve, base_bits + k), swapped(side, base_bits + k)
        solves.append(sib_solve)
        sides.append(sib_side)
        rows = solve.shape[0] - solve_rows(k, levels, rank)
        out_shape = [jax.ShapeDtypeStruct((order, half), F32)]
        if rows:
            out_shape.append(jax.ShapeDtypeStruct((rows, half), F32))
        outs = pl.pallas_call(
            functools.partial(level_kernel, (levels, rank, base_bits), k),
            out_shape=out_shape,
            in_specs=[vmem] * 3,
            out_specs=[vmem] * len(out_shape),
            compiler_params=small,
            cost_estimate=pl.CostEstimate(flops=2 * 10**10, bytes_accessed=2 * MIB, transcendentals=0),
            name=f"level_{k}",
        )(solve, sib_solve, nodes)
        zs.append(outs[0])
        if rows:
            solve = outs[1]
            start = side_rows(k, levels, rank)
            side = pl.pallas_call(
                functools.partial(side_sum_kernel, start),
                out_shape=jax.ShapeDtypeStruct((side.shape[0] - start, half), F32),
                in_specs=[vmem] * 3,
                out_specs=vmem,
                compiler_params=small,
                name=f"side_sum_{k}",
            )(side, sib_side, outs[0])

    pair = base_bits == 0
    ends = [*solves, *sides, *zs] + ([first_solve, first_side] if pair else [])
    *send, own = pl.pallas_call(
        functools.partial(end_kernel, (levels, rank), 1.0 / col_count**0.5, pair),
        out_shape=[jax.ShapeDtypeStruct((3 * wide, half), F32)] * (2 if pair else 1),
        in_specs=[vmem] * len(ends),
        out_specs=[vmem] * (2 if pair else 1),
        compiler_params=small,
        name="end_factors",
    )(*ends)
    other = swapped(send[0] if pair else own, 0)

    sol, left, right = pl.pallas_call(
        functools.partial(final_kernel, chunk),
        grid=(steps,),
        out_shape=[
            jax.ShapeDtypeStruct((row_count, col_count), F32),
            jax.ShapeDtypeStruct((wide, row_count), jnp.bfloat16),
            jax.ShapeDtypeStruct((wide, row_count), jnp.bfloat16),
        ],
        in_specs=[smem, fixed(3 * wide, half), fixed(3 * wide, half), by_row, by_row, by_lane],
        out_specs=[by_row, by_lane, by_lane],
        compiler_params=params,
        name="row_outputs",
    )(leaf_rows, own, other, right_side, cotangent, q_all)
    return sol, left.reshape(coeff_basis.shape), right.reshape(coeff_basis.shape)


def solution(mesh):
    in_specs = (
        P(("groups", "leaf"), None),
        P(("groups", "leaf"), None),
        P(None, None, ("groups", "leaf")),
        P(None, None, ("groups", "leaf")),
        P("groups", None, None),
        P(("groups", "leaf")),
    )
    out_specs = (
        P(("groups", "leaf"), None),
        P(None, None, ("groups", "leaf")),
        P(None, None, ("groups", "leaf")),
    )
    return jax.shard_map(body, mesh=mesh, in_specs=in_specs, out_specs=out_specs, check_vma=False)
```

```python
import functools

import jax
import jax.numpy as jnp
from jax import lax
from jax.experimental import pallas as pl
from jax.experimental.pallas import tpu as pltpu
from jax.sharding import PartitionSpec as P


HIGH = lax.Precision.HIGH
F32 = jnp.float32
MIB = 2**20


def dot(a, b, dims=((1,), (0,))):
    return lax.dot_general(a, b, (dims, ((), ())), precision=HIGH, preferred_element_type=F32)


def pack(blocks):
    rows = []
    for i in range(0, len(blocks) - 1, 2):
        rows.append(jnp.concatenate([blocks[i], blocks[i + 1]], 1))
    if len(blocks) % 2:
        half = blocks[-1].shape[0] // 2
        rows.append(jnp.concatenate([blocks[-1][:half], blocks[-1][half:]], 1))
    return rows


def pack_rows(count, rank):
    return count // 2 * rank + count % 2 * (rank // 2)


def unpack(ref, start, count, rank):
    blocks = []
    for i in range(count):
        if i == count - 1 and count % 2:
            half = ref[start : start + rank // 2, :]
            blocks.append(jnp.concatenate([half[:, :rank], half[:, rank:]], 0))
        else:
            lane = i % 2 * rank
            blocks.append(ref[start : start + rank, lane : lane + rank])
            start += i % 2 * rank
    return blocks


def side_rows(level, levels, rank):
    return rank + pack_rows(levels - level, rank)


def solve_rows(level, levels, rank):
    return rank + pack_rows(levels - 1 - level, rank)


def write_state(keep, send, acc, rank, blocks_of):
    half = acc.shape[1] // 2
    is_first = lax.axis_index("leaf") % 2 == 0
    at = 0
    for k in range(acc.shape[0] // rank):
        low = acc[k * rank : (k + 1) * rank, :half]
        high = acc[k * rank : (k + 1) * rank, half:]
        keep[at : at + rank, :] = jnp.where(is_first, low, high)
        send[at : at + rank, :] = jnp.where(is_first, high, low)
        at += rank
        for rows in pack(blocks_of(k)):
            keep[at : at + rows.shape[0], :] = rows
            send[at : at + rows.shape[0], :] = rows
            at += rows.shape[0]


def local_kernel(dims, rows_hbm, x_hbm, w_hbm, u_hbm, q_hbm, node_ref, *refs):
    levels, rank, base_bits, chunk, ahead = dims
    keep, send, g_ref, nodes_out, count_out, x_all, w_all, u_all, q_all = refs[:9]
    rows_ref, c_acc, sems, w_sem, row_sem, node_sems = refs[9:]
    position = lax.axis_index("leaf")
    steps = x_all.shape[0] // chunk

    def copies(i):
        part = pl.ds(pl.multiple_of(i * chunk, chunk), chunk)
        pairs = [(u_hbm.at[:, part], u_all.at[:, part]), (x_hbm.at[part], x_all.at[part])]
        pairs.append((q_hbm.at[:, part], q_all.at[:, part]))
        return [pltpu.make_async_copy(a, b, sems.at[i, n]) for n, (a, b) in enumerate(pairs)]

    def node_copy(k):
        index = 2**levels - 2 ** (levels - k) + jnp.right_shift(position, base_bits + k + 1)
        return pltpu.make_async_copy(node_ref.at[index], nodes_out.at[k], node_sems.at[k])

    row_copy = pltpu.make_async_copy(rows_hbm, rows_ref, row_sem)
    w_copy = pltpu.make_async_copy(w_hbm, w_all, w_sem)
    row_copy.start()
    for i in range(min(ahead, steps)):
        for copy in copies(i):
            copy.start()
    for k in range(levels):
        node_copy(k).start()
    c_acc[...] = jnp.zeros_like(c_acc)
    g_ref[...] = jnp.zeros_like(g_ref)
    row_copy.wait()
    count_out[...] = jnp.full(count_out.shape, rows_ref[0], jnp.int32)

    def step(i, carry):
        @pl.when(i + ahead < steps)
        def _():
            for copy in copies(i + ahead):
                copy.start()

        @pl.when(i + ahead == max(steps, ahead))
        def _():
            w_copy.start()

        for copy in copies(i):
            copy.wait()
        part = pl.ds(pl.multiple_of(i * chunk, chunk), chunk)
        place = i * chunk + lax.broadcasted_iota(jnp.int32, (1, chunk), 1)
        u = jnp.where(place < rows_ref[0], u_all[:, part], 0.0)
        c_acc[...] += dot(u, x_all[part, :])
        g_ref[...] += dot(u, q_all[:, part], ((1,), (1,)))
        return carry

    lax.fori_loop(0, steps, step, 0)

    def blocks(k):
        lane = slice(k * rank, (k + 1) * rank)
        return [g_ref[i * rank : (i + 1) * rank, lane] for i in range(k + 1, levels)]

    write_state(keep, send, c_acc, rank, blocks)
    for k in range(levels):
        node_copy(k).wait()
    w_copy.wait()


def side_kernel(dims, count_ref, w_ref, u_ref, g_ref, keep, send, k_acc):
    levels, rank = dims
    place = lax.broadcasted_iota(jnp.int32, (1, u_ref.shape[1]), 1)
    u = jnp.where(place < count_ref[:1, :1], u_ref[...], 0.0)
    k_acc[...] = dot(u, w_ref[...])

    def blocks(k):
        row = slice(k * rank, (k + 1) * rank)
        return [g_ref[row, j * rank : (j + 1) * rank] for j in range(k, levels)]

    write_state(keep, send, k_acc, rank, blocks)


def side_first_kernel(at, own_ref, sib_ref, after_ref, *out_refs):
    del after_ref
    for out_ref in out_refs:
        rows = out_ref.shape[0]
        out_ref[...] = own_ref[at : at + rows, :] + sib_ref[at : at + rows, :]
        at += rows


def side_join_kernel(first, fresh_ref, sent_ref, got_ref, after_ref, out_ref):
    del after_ref
    rows = fresh_ref.shape[0]
    out_ref[:rows, :] = fresh_ref[...]
    out_ref[rows : rows + first, :] = got_ref[:first, :]
    out_ref[rows + first :, :] = sent_ref[first:, :] + got_ref[first:, :]


def side_top_kernel(sent_ref, got_ref, after_ref, out_ref):
    del after_ref
    at = sent_ref.shape[0] - out_ref.shape[0]
    out_ref[...] = sent_ref[at:, :] + got_ref[at:, :]


def level_kernel(dims, level, own_ref, sib_ref, nodes_ref, *refs):
    levels, rank, base_bits, placed = dims
    z_ref, *out_refs = refs[1:] if placed else refs
    is_lower = jnp.right_shift(lax.axis_index("leaf"), base_bits + level) % 2 == 0
    own, sib = own_ref[:rank, :], sib_ref[:rank, :]
    both = jnp.concatenate([jnp.where(is_lower, own, sib), jnp.where(is_lower, sib, own)], 0)
    mixed = dot(nodes_ref[level], both)
    z_own = jnp.where(is_lower, mixed[:rank], mixed[rank:])
    z_sib = jnp.where(is_lower, mixed[rank:], mixed[:rank])
    z_ref[:rank, :] = z_own
    z_ref[rank:, :] = z_sib
    if not out_refs:
        return
    (out_ref,) = out_refs
    count = levels - 1 - level
    h_own = unpack(own_ref, rank, count, rank)
    h_sib = unpack(sib_ref, rank, count, rank)
    h_both = jnp.concatenate([jnp.concatenate(h_own, 0), jnp.concatenate(h_sib, 0)], 1)
    drop = dot(h_both, jnp.concatenate([z_own, z_sib], 0))

    def total(at, rows):
        return own_ref[at : at + rows, :] + sib_ref[at : at + rows, :]

    start = solve_rows(level, levels, rank)
    at = 0
    for i in range(count):
        out_ref[at : at + rank, :] = total(start + at, rank) - drop[i * rank : (i + 1) * rank]
        at += rank
        rest = solve_rows(level + 1 + i, levels, rank) - rank
        if rest:
            out_ref[at : at + rest, :] = total(start + at, rest)
            at += rest


def factor_terms(dims, k, c, side_ref, at, z_here, z_above):
    levels, rank, scale = dims
    blocks = unpack(side_ref, at + rank, levels - k, rank)
    z_here = jnp.concatenate([z_here, *z_above], 0)
    l_term = c - dot(jnp.concatenate(blocks, 1), z_here)
    return l_term * scale, side_ref[at : at + rank, :] * scale


def end_low_kernel(dims, pair, *refs):
    levels, rank, scale = dims
    z_refs, (sib_side, side_sent, side_got, own_side) = refs[:levels], refs[levels : levels + 4]
    out_refs = refs[levels + 4 :]
    for n, out_ref in enumerate(out_refs):
        crossed = pair and n == 0
        at = 0
        for k in range(levels):
            z = z_refs[k][rank:, :] if crossed and k == 0 else z_refs[k][:rank, :]
            out_ref[k * rank : (k + 1) * rank, :] = z
            if k == levels - 1:
                continue
            if k == 0:
                term = (own_side if crossed else sib_side)[:rank, :]
            else:
                term = side_got[at : at + rank, :]
                if k > 1:
                    term = term + side_sent[at : at + rank, :]
                at += side_rows(k, levels, rank)
            out_ref[(levels + k) * rank : (levels + k + 1) * rank, :] = term * scale


def end_kernel(dims, pair, *refs):
    levels, rank, _ = dims
    solves, z_refs = refs[:levels], refs[levels : 2 * levels]
    sib_side, side_sent, side_got, top_side, own_solve, own_side = refs[2 * levels : 2 * levels + 6]
    *out_refs, side_sum = refs[2 * levels + 6 :]
    z_own = [z_ref[:rank, :] for z_ref in z_refs]

    low = side_rows(1, levels, rank)
    rows = side_sum.shape[0]
    side_sum[:low, :] = side_got[:low, :]
    side_sum[low:, :] = side_got[low:rows, :] + side_sent[low:rows, :]
    at = 0
    for k in range(levels):
        where = (side_sum, at)
        if k == 0:
            where = (sib_side, 0)
        elif k == levels - 1:
            where = (top_side, 0)
        else:
            at += side_rows(k, levels, rank)
        l_term, k_term = factor_terms(dims, k, solves[k][:rank, :], *where, z_refs[k][rank:, :], z_own[k + 1 :])
        out_refs[-1][k * rank : (k + 1) * rank, :] = l_term
        if pair:
            if k == 0:
                l_term, _ = factor_terms(dims, 0, own_solve[:rank, :], own_side, 0, z_own[0], z_own[1:])
            out_refs[0][k * rank : (k + 1) * rank, :] = l_term
    for out_ref in out_refs:
        out_ref[levels * rank :, :] = k_term


def whole(own_ref, other_ref, start, rows):
    is_first = lax.axis_index("leaf") % 2 == 0
    own, other = own_ref[start : start + rows, :], other_ref[start : start + rows, :]
    return jnp.concatenate([jnp.where(is_first, own, other), jnp.where(is_first, other, own)], 1)


class Sender:
    def __init__(self, sems):
        self.sems, self.copies = sems, []

    def send(self, source, target):
        copy = pltpu.make_async_copy(source, target, self.sems.at[len(self.copies)])
        copy.start()
        self.copies.append(copy)

    def wait(self):
        for copy in self.copies:
            copy.wait()


def solution_kernel(dims, count_ref, own_ref, other_ref, x_ref, q_ref, sol):
    wide, chunk = dims
    z = whole(own_ref, other_ref, 0, wide)
    for i in range(x_ref.shape[0] // chunk):
        part = slice(i * chunk, (i + 1) * chunk)
        live = i * chunk + lax.broadcasted_iota(jnp.int32, (chunk, 1), 0) < count_ref[:1, :1]
        x = x_ref[part, :] - dot(q_ref[:, part], z, ((0,), (0,)))
        sol[part, :] = jnp.where(live, x, 0.0)


def factor_kernel(dims, count_ref, low_own, low_other, top_own, top_other, x_ref, w_ref, *refs):
    wide, chunk = dims
    sol_out, left_out, right_out, left, right, sems = refs
    sender = Sender(sems)
    sender.send(x_ref, sol_out)
    low = low_own.shape[0] - wide
    l = whole(top_own, top_other, 0, wide)
    k = jnp.concatenate([whole(low_own, low_other, wide, low), whole(top_own, top_other, wide, wide - low)], 0)
    for i in range(x_ref.shape[0] // chunk):
        part, place = slice(i * chunk, (i + 1) * chunk), pl.ds(i * chunk, chunk)
        live = i * chunk + lax.broadcasted_iota(jnp.int32, (1, chunk), 1) < count_ref[:1, :1]
        left_now = dot(l, w_ref[part, :], ((1,), (1,)))
        left[:, part] = jnp.where(live, left_now, 0.0).astype(left.dtype)
        sender.send(left.at[:, place], left_out.at[:, place])
        right[:, part] = dot(k, x_ref[part, :], ((1,), (1,))).astype(right.dtype)
        sender.send(right.at[:, place], right_out.at[:, place])
    sender.wait()


def swapped(value, bit):
    mask = 2**bit
    pairs = [(source, source ^ mask) for source in range(lax.axis_size("leaf"))]
    return lax.ppermute(value, "leaf", pairs)


def shape(*sizes, dtype=F32):
    return jax.ShapeDtypeStruct(sizes, dtype)


def body(right_side, cotangent, coeff_basis, saved_basis, node_inverse, leaf_rows):
    row_count, col_count = right_side.shape
    levels, rank = coeff_basis.shape[:2]
    wide, order, half = levels * rank, 2 * rank, col_count // 2
    low, top = wide - rank, levels - 1
    base_bits = lax.axis_size("leaf").bit_length() - 1 - levels
    pair = base_bits == 0
    chunk = min(512, row_count)
    steps = row_count // chunk
    u_all = coeff_basis.reshape(wide, row_count)
    q_all = saved_basis.reshape(wide, row_count)

    vmem = pl.BlockSpec(memory_space=pltpu.VMEM)
    anywhere = pl.BlockSpec(memory_space=pl.ANY)
    small = pltpu.CompilerParams(vmem_limit_bytes=4 * MIB)
    large = pltpu.CompilerParams(vmem_limit_bytes=20 * MIB)

    def call(kernel, name, out_shape, *operands, out_specs=vmem, scratch=(), params=small, cost=None, **options):
        if isinstance(out_shape, list) and out_specs is vmem:
            out_specs = [vmem] * len(out_shape)
        if cost is not None:
            options["cost_estimate"] = pl.CostEstimate(flops=cost, bytes_accessed=MIB, transcendentals=0)
        return pl.pallas_call(
            kernel,
            out_shape=out_shape,
            in_specs=[vmem] * len(operands),
            out_specs=out_specs,
            scratch_shapes=list(scratch),
            compiler_params=params,
            name=name,
            **options,
        )(*operands)

    n_solve = sum(solve_rows(k, levels, rank) for k in range(levels))
    n_side = [side_rows(k, levels, rank) for k in range(levels)]
    arrays = (right_side, cotangent, u_all, q_all)
    outs = [shape(n_solve, half), shape(n_solve, half), shape(wide, wide), shape(levels, order, order)]
    outs += [shape(8, 128, dtype=jnp.int32)] + [shape(*a.shape) for a in arrays]
    hbm = [pltpu.with_memory_space_constraint(a, pltpu.HBM) for a in (*arrays, node_inverse)]
    solve, solve_send, products, nodes, count, x_vmem, w_vmem, u_vmem, q_vmem = pl.pallas_call(
        functools.partial(local_kernel, (levels, rank, base_bits, chunk, 2)),
        out_shape=outs,
        in_specs=[anywhere] * 6,
        out_specs=[vmem] * 9,
        scratch_shapes=[
            pltpu.SMEM((1,), jnp.int32),
            pltpu.VMEM((wide, col_count), F32),
            pltpu.SemaphoreType.DMA((steps, 3)),
            pltpu.SemaphoreType.DMA,
            pltpu.SemaphoreType.DMA,
            pltpu.SemaphoreType.DMA((levels,)),
        ],
        compiler_params=large,
        name="local_sums",
    )(leaf_rows, *hbm)
    side, side_send = call(
        functools.partial(side_kernel, (levels, rank)),
        "side_sums",
        [shape(sum(n_side), half)] * 2,
        count,
        w_vmem,
        u_vmem,
        products,
        scratch=[pltpu.VMEM((wide, col_count), F32)],
        params=large,
        cost=6 * wide * row_count * col_count,
    )

    if pair:
        sib_solve, sib_side = swapped(solve_send, 0), swapped(side_send, 0)
    else:
        solve, side = solve + swapped(solve_send, 0), side + swapped(side_send, 0)
        for bit in range(1, base_bits):
            solve, side = solve + swapped(solve, bit), side + swapped(side, bit)
        sib_solve, sib_side = swapped(solve, base_bits), swapped(side, base_bits)

    own_solve = solve
    solves, zs, fresh, placed = [], [], {}, []
    sent = got = None
    for k in range(levels):
        if k > 0:
            sib_solve = swapped(solve, base_bits + k)
        solves.append(sib_solve)
        out_shape = [shape(order, half)]
        if k < top:
            out_shape.append(shape(sum(solve_rows(i, levels, rank) for i in range(k + 1, levels)), half))
        outs = call(
            functools.partial(level_kernel, (levels, rank, base_bits, len(placed) > 0), k),
            f"level_{k}",
            out_shape,
            solve,
            sib_solve,
            nodes,
            *placed,
            cost=2 * 10**10,
        )
        zs.append(outs[0])
        if k < top:
            solve = outs[1]
        if k == 0:
            sizes = [*n_side[1 : top - 1], n_side[top - 1] + n_side[top]]
            first = call(
                functools.partial(side_first_kernel, n_side[0]),
                "side_first",
                [shape(size, half) for size in sizes],
                side,
                sib_side,
                outs[0],
            )
            fresh = dict(enumerate(first, 1))
            sent = fresh[top - 1]
            got = swapped(sent, base_bits + top - 1)
        elif k < top - 1:
            bit = top - 1 - k
            sent = call(
                functools.partial(side_join_kernel, n_side[bit + 1]),
                f"side_join_{bit}",
                shape(fresh[bit].shape[0] + sent.shape[0], half),
                fresh[bit],
                sent,
                got,
                outs[0],
            )
            got = swapped(sent, base_bits + bit)
            placed = [sent]
        elif k == top - 1:
            last = call(side_top_kernel, "side_top", shape(n_side[top], half), sent, got, outs[0])
            placed = [last]
    top_side = swapped(last, base_bits + top)

    dims = (levels, rank, 1.0 / col_count**0.5)
    copies = 2 if pair else 1
    *low_other, low_own = call(
        functools.partial(end_low_kernel, dims, pair),
        "end_low",
        [shape(wide + low, half)] * copies,
        *zs,
        sib_side,
        sent,
        got,
        side,
    )
    low_other = swapped(low_other[0] if pair else low_own, 0)
    *top_other, top_own = call(
        functools.partial(end_kernel, dims, pair),
        "end_factors",
        [shape(wide + rank, half)] * copies,
        *solves,
        *zs,
        sib_side,
        sent,
        got,
        top_side,
        own_solve,
        side,
        scratch=[pltpu.VMEM((sum(n_side[1:top]), half), F32)],
        cost=2 * 10**10,
    )
    top_other = swapped(top_other[0] if pair else top_own, 0)

    sol_vmem = call(
        functools.partial(solution_kernel, (wide, chunk)),
        "solution_rows",
        shape(row_count, col_count),
        count,
        low_own,
        low_other,
        x_vmem,
        q_vmem,
        params=large,
        cost=2 * 10**9,
    )
    grad = shape(wide, row_count, dtype=jnp.bfloat16)
    sol, left, right = call(
        functools.partial(factor_kernel, (wide, chunk)),
        "factor_rows",
        [shape(row_count, col_count), grad, grad],
        count,
        low_own,
        low_other,
        top_own,
        top_other,
        sol_vmem,
        w_vmem,
        out_specs=[anywhere] * 3,
        scratch=[pltpu.VMEM(grad.shape, grad.dtype)] * 2 + [pltpu.SemaphoreType.DMA((2 * steps + 1,))],
        params=large,
    )
    return sol, left.reshape(coeff_basis.shape), right.reshape(coeff_basis.shape)


def solution(mesh):
    in_specs = (
        P(("groups", "leaf"), None),
        P(("groups", "leaf"), None),
        P(None, None, ("groups", "leaf")),
        P(None, None, ("groups", "leaf")),
        P("groups", None, None),
        P(("groups", "leaf")),
    )
    out_specs = (
        P(("groups", "leaf"), None),
        P(None, None, ("groups", "leaf")),
        P(None, None, ("groups", "leaf")),
    )
    return jax.shard_map(body, mesh=mesh, in_specs=in_specs, out_specs=out_specs, check_vma=False)
```

```python
import functools

import jax
import jax.numpy as jnp
from jax import lax
from jax.experimental import pallas as pl
from jax.experimental.pallas import tpu as pltpu
from jax.sharding import PartitionSpec as P


HIGH = lax.Precision.HIGH
F32 = jnp.float32
MIB = 2**20


def dot(a, b, dims=((1,), (0,))):
    return lax.dot_general(a, b, (dims, ((), ())), precision=HIGH, preferred_element_type=F32)


def pack(blocks):
    rows = []
    for i in range(0, len(blocks) - 1, 2):
        rows.append(jnp.concatenate([blocks[i], blocks[i + 1]], 1))
    if len(blocks) % 2:
        half = blocks[-1].shape[0] // 2
        rows.append(jnp.concatenate([blocks[-1][:half], blocks[-1][half:]], 1))
    return rows


def pack_rows(count, rank):
    return count // 2 * rank + count % 2 * (rank // 2)


def unpack(ref, start, count, rank):
    blocks = []
    for i in range(count):
        if i == count - 1 and count % 2:
            half = ref[start : start + rank // 2, :]
            blocks.append(jnp.concatenate([half[:, :rank], half[:, rank:]], 0))
        else:
            lane = i % 2 * rank
            blocks.append(ref[start : start + rank, lane : lane + rank])
            start += i % 2 * rank
    return blocks


def side_rows(level, levels, rank):
    return rank + pack_rows(levels - level, rank)


def solve_rows(level, levels, rank):
    return rank + pack_rows(levels - 1 - level, rank)


def row_parts(row_count):
    eighth = row_count // 8
    if eighth % 128:
        return [(0, row_count)]
    sizes = [eighth, 2 * eighth, 2 * eighth, 2 * eighth, eighth]
    return [(sum(sizes[:n]), size) for n, size in enumerate(sizes)]


def write_state(keep, send, acc, rank, blocks_of):
    half = acc.shape[1] // 2
    is_first = lax.axis_index("leaf") % 2 == 0
    at = 0
    for k in range(acc.shape[0] // rank):
        low = acc[k * rank : (k + 1) * rank, :half]
        high = acc[k * rank : (k + 1) * rank, half:]
        keep[at : at + rank, :] = jnp.where(is_first, low, high)
        send[at : at + rank, :] = jnp.where(is_first, high, low)
        at += rank
        for rows in pack(blocks_of(k)):
            keep[at : at + rows.shape[0], :] = rows
            send[at : at + rows.shape[0], :] = rows
            at += rows.shape[0]


def local_kernel(dims, parts, ahead, count_ref, x_hbm, w_hbm, u_hbm, q_hbm, node_ref, *refs):
    levels, rank, base_bits = dims
    keep, send, g_ref, nodes_out, x_all, w_all, u_all, q_all, c_acc, sems, w_sem, node_sems = refs
    position = lax.axis_index("leaf")

    def copies(n):
        part = pl.ds(*parts[n])
        pairs = [(u_hbm.at[:, part], u_all.at[:, part]), (x_hbm.at[part], x_all.at[part])]
        pairs.append((q_hbm.at[:, part], q_all.at[:, part]))
        return [pltpu.make_async_copy(a, b, sems.at[n, i]) for i, (a, b) in enumerate(pairs)]

    def node_copy(k):
        index = 2**levels - 2 ** (levels - k) + jnp.right_shift(position, base_bits + k + 1)
        return pltpu.make_async_copy(node_ref.at[index], nodes_out.at[k], node_sems.at[k])

    w_copy = pltpu.make_async_copy(w_hbm, w_all, w_sem)
    for n in range(ahead):
        for copy in copies(n):
            copy.start()
    for k in range(levels):
        node_copy(k).start()

    for n, (first, size) in enumerate(parts):
        @pl.when(position >= 0)
        def _():
            if n + ahead < len(parts):
                for copy in copies(n + ahead):
                    copy.start()
            if n + ahead == len(parts):
                w_copy.start()
            for copy in copies(n):
                copy.wait()
            part = pl.ds(first, size)
            place = first + lax.broadcasted_iota(jnp.int32, (1, size), 1)
            u = jnp.where(place < count_ref[:1, :1], u_all[:, part], 0.0)
            c = dot(u, x_all[part, :])
            g = dot(u, q_all[:, part], ((1,), (1,)))
            c_acc[...] = c if n == 0 else c_acc[...] + c
            g_ref[...] = g if n == 0 else g_ref[...] + g

    def blocks(k):
        lane = slice(k * rank, (k + 1) * rank)
        return [g_ref[i * rank : (i + 1) * rank, lane] for i in range(k + 1, levels)]

    write_state(keep, send, c_acc, rank, blocks)
    for k in range(levels):
        node_copy(k).wait()
    w_copy.wait()


def side_kernel(count_ref, w_ref, u_ref, k_ref):
    place = lax.broadcasted_iota(jnp.int32, (1, u_ref.shape[1]), 1)
    k_ref[...] = dot(jnp.where(place < count_ref[:1, :1], u_ref[...], 0.0), w_ref[...])


def side_state_kernel(dims, k_ref, g_ref, after_ref, keep, send):
    del after_ref
    levels, rank = dims

    def blocks(k):
        row = slice(k * rank, (k + 1) * rank)
        return [g_ref[row, j * rank : (j + 1) * rank] for j in range(k, levels)]

    write_state(keep, send, k_ref, rank, blocks)


def side_first_kernel(at, own_ref, sib_ref, after_ref, *out_refs):
    del after_ref
    for out_ref in out_refs:
        rows = out_ref.shape[0]
        out_ref[...] = own_ref[at : at + rows, :] + sib_ref[at : at + rows, :]
        at += rows


def side_join_kernel(first, fresh_ref, sent_ref, got_ref, after_ref, *refs):
    del after_ref
    *top_ref, out_ref = refs
    at, rows = fresh_ref.shape[0], got_ref.shape[0]
    out_ref[:at, :] = fresh_ref[...]
    out_ref[at : at + first, :] = got_ref[:first, :]
    if first < rows:
        out_ref[at + first : at + rows, :] = sent_ref[first:, :] + got_ref[first:, :]
    if top_ref:
        out_ref[at + rows :, :] = top_ref[0][...]


def side_top_kernel(sent_ref, got_ref, after_ref, out_ref):
    del after_ref
    at = sent_ref.shape[0] - out_ref.shape[0]
    out_ref[...] = sent_ref[at:, :] + got_ref[at:, :]


def level_kernel(dims, level, own_ref, sib_ref, nodes_ref, *refs):
    levels, rank, base_bits, placed = dims
    z_ref, *out_refs = refs[placed:]
    is_lower = jnp.right_shift(lax.axis_index("leaf"), base_bits + level) % 2 == 0
    own, sib = own_ref[:rank, :], sib_ref[:rank, :]
    both = jnp.concatenate([jnp.where(is_lower, own, sib), jnp.where(is_lower, sib, own)], 0)
    mixed = dot(nodes_ref[level], both)
    z_own = jnp.where(is_lower, mixed[:rank], mixed[rank:])
    z_sib = jnp.where(is_lower, mixed[rank:], mixed[:rank])
    z_ref[:rank, :] = z_own
    z_ref[rank:, :] = z_sib
    if not out_refs:
        return
    (out_ref,) = out_refs
    count = levels - 1 - level
    h_own = unpack(own_ref, rank, count, rank)
    h_sib = unpack(sib_ref, rank, count, rank)
    h_both = jnp.concatenate([jnp.concatenate(h_own, 0), jnp.concatenate(h_sib, 0)], 1)
    drop = dot(h_both, jnp.concatenate([z_own, z_sib], 0))

    def total(at, rows):
        return own_ref[at : at + rows, :] + sib_ref[at : at + rows, :]

    start = solve_rows(level, levels, rank)
    at = 0
    for i in range(count):
        out_ref[at : at + rank, :] = total(start + at, rank) - drop[i * rank : (i + 1) * rank]
        at += rank
        rest = solve_rows(level + 1 + i, levels, rank) - rank
        if rest:
            out_ref[at : at + rest, :] = total(start + at, rest)
            at += rest


def factor_terms(dims, k, c, side_ref, at, z_here, z_above):
    levels, rank, scale = dims
    blocks = unpack(side_ref, at + rank, levels - k, rank)
    z_here = jnp.concatenate([z_here, *z_above], 0)
    l_term = c - dot(jnp.concatenate(blocks, 1), z_here)
    return l_term * scale, side_ref[at : at + rank, :] * scale


def end_low_kernel(dims, pair, *refs):
    levels, rank, scale = dims
    z_refs, (sib_side, side_sent, side_got, own_side) = refs[:levels], refs[levels : levels + 4]
    out_refs = refs[levels + 4 :]
    for n, out_ref in enumerate(out_refs):
        crossed = pair and n == 0
        at = 0
        for k in range(levels):
            z = z_refs[k][rank:, :] if crossed and k == 0 else z_refs[k][:rank, :]
            out_ref[k * rank : (k + 1) * rank, :] = z
            if k == levels - 1:
                continue
            if k == 0:
                term = (own_side if crossed else sib_side)[:rank, :]
            else:
                term = side_got[at : at + rank, :]
                if k > 1:
                    term = term + side_sent[at : at + rank, :]
                at += side_rows(k, levels, rank)
            out_ref[(levels + k) * rank : (levels + k + 1) * rank, :] = term * scale


def end_kernel(dims, pair, *refs):
    levels, rank, _ = dims
    solves, z_refs = refs[:levels], refs[levels : 2 * levels]
    sib_side, side_sent, side_got, top_sent, top_got, own_solve, own_side = refs[2 * levels : 2 * levels + 7]
    *out_refs, side_sum, top_side = refs[2 * levels + 7 :]
    top_side[...] = top_sent[...] + top_got[...]
    z_own = [z_ref[:rank, :] for z_ref in z_refs]

    low = side_rows(1, levels, rank)
    rows = side_sum.shape[0]
    side_sum[:low, :] = side_got[:low, :]
    side_sum[low:, :] = side_got[low:rows, :] + side_sent[low:rows, :]
    at = 0
    for k in range(levels):
        where = (side_sum, at)
        if k == 0:
            where = (sib_side, 0)
        elif k == levels - 1:
            where = (top_side, 0)
        else:
            at += side_rows(k, levels, rank)
        l_term, k_term = factor_terms(dims, k, solves[k][:rank, :], *where, z_refs[k][rank:, :], z_own[k + 1 :])
        out_refs[-1][k * rank : (k + 1) * rank, :] = l_term
        if pair:
            if k == 0:
                l_term, _ = factor_terms(dims, 0, own_solve[:rank, :], own_side, 0, z_own[0], z_own[1:])
            out_refs[0][k * rank : (k + 1) * rank, :] = l_term
    for out_ref in out_refs:
        out_ref[levels * rank :, :] = k_term


def whole(own_ref, other_ref, start, rows):
    is_first = lax.axis_index("leaf") % 2 == 0
    own, other = own_ref[start : start + rows, :], other_ref[start : start + rows, :]
    return jnp.concatenate([jnp.where(is_first, own, other), jnp.where(is_first, other, own)], 1)


class Sender:
    def __init__(self, sems):
        self.sems, self.copies = sems, []

    def send(self, source, target):
        copy = pltpu.make_async_copy(source, target, self.sems.at[len(self.copies)])
        copy.start()
        self.copies.append(copy)

    def wait(self):
        for copy in self.copies:
            copy.wait()


def solution_kernel(dims, count_ref, own_ref, other_ref, x_ref, q_ref, sol):
    wide, chunk = dims
    z = whole(own_ref, other_ref, 0, wide)
    for i in range(x_ref.shape[0] // chunk):
        part = slice(i * chunk, (i + 1) * chunk)
        live = i * chunk + lax.broadcasted_iota(jnp.int32, (chunk, 1), 0) < count_ref[:1, :1]
        x = x_ref[part, :] - dot(q_ref[:, part], z, ((0,), (0,)))
        sol[part, :] = jnp.where(live, x, 0.0)


def factor_kernel(dims, count_ref, low_own, low_other, top_own, top_other, x_ref, w_ref, *refs):
    wide, chunk = dims
    sol_out, left_out, right_out, left, right, sems = refs
    sender = Sender(sems)
    sender.send(x_ref, sol_out)
    low = low_own.shape[0] - wide
    l = whole(top_own, top_other, 0, wide)
    k = jnp.concatenate([whole(low_own, low_other, wide, low), whole(top_own, top_other, wide, wide - low)], 0)
    for i in range(x_ref.shape[0] // chunk):
        part, place = slice(i * chunk, (i + 1) * chunk), pl.ds(i * chunk, chunk)
        live = i * chunk + lax.broadcasted_iota(jnp.int32, (1, chunk), 1) < count_ref[:1, :1]
        left_now = dot(l, w_ref[part, :], ((1,), (1,)))
        left[:, part] = jnp.where(live, left_now, 0.0).astype(left.dtype)
        sender.send(left.at[:, place], left_out.at[:, place])
        right[:, part] = dot(k, x_ref[part, :], ((1,), (1,))).astype(right.dtype)
        sender.send(right.at[:, place], right_out.at[:, place])
    sender.wait()


def swapped(value, bit):
    mask = 2**bit
    pairs = [(source, source ^ mask) for source in range(lax.axis_size("leaf"))]
    return lax.ppermute(value, "leaf", pairs)


def shape(*sizes, dtype=F32):
    return jax.ShapeDtypeStruct(sizes, dtype)


def body(right_side, cotangent, coeff_basis, saved_basis, node_inverse, leaf_rows):
    row_count, col_count = right_side.shape
    levels, rank = coeff_basis.shape[:2]
    wide, order, half = levels * rank, 2 * rank, col_count // 2
    low, top = wide - rank, levels - 1
    base_bits = lax.axis_size("leaf").bit_length() - 1 - levels
    pair = base_bits == 0
    chunk = min(512, row_count)
    steps = row_count // chunk
    parts = row_parts(row_count)
    u_all = coeff_basis.reshape(wide, row_count)
    q_all = saved_basis.reshape(wide, row_count)

    vmem = pl.BlockSpec(memory_space=pltpu.VMEM)
    anywhere = pl.BlockSpec(memory_space=pl.ANY)
    small = pltpu.CompilerParams(vmem_limit_bytes=4 * MIB)
    large = pltpu.CompilerParams(vmem_limit_bytes=20 * MIB)

    def call(kernel, name, out_shape, *operands, out_specs=vmem, scratch=(), params=small, cost=None, **options):
        if isinstance(out_shape, list) and out_specs is vmem:
            out_specs = [vmem] * len(out_shape)
        if cost is not None:
            options["cost_estimate"] = pl.CostEstimate(flops=cost, bytes_accessed=MIB, transcendentals=0)
        return pl.pallas_call(
            kernel,
            out_shape=out_shape,
            in_specs=[vmem] * len(operands),
            out_specs=out_specs,
            scratch_shapes=list(scratch),
            compiler_params=params,
            name=name,
            **options,
        )(*operands)

    n_solve = sum(solve_rows(k, levels, rank) for k in range(levels))
    n_side = [side_rows(k, levels, rank) for k in range(levels)]
    arrays = (right_side, cotangent, u_all, q_all)
    outs = [shape(n_solve, half), shape(n_solve, half), shape(wide, wide), shape(levels, order, order)]
    outs += [shape(*a.shape) for a in arrays]
    count = jnp.broadcast_to(leaf_rows[:, None], (8, 128))
    hbm = [pltpu.with_memory_space_constraint(a, pltpu.HBM) for a in (*arrays, node_inverse)]
    solve, solve_send, products, nodes, x_vmem, w_vmem, u_vmem, q_vmem = pl.pallas_call(
        functools.partial(local_kernel, (levels, rank, base_bits), parts, min(3, len(parts))),
        out_shape=outs,
        in_specs=[vmem] + [anywhere] * 5,
        out_specs=[vmem] * 8,
        scratch_shapes=[
            pltpu.VMEM((wide, col_count), F32),
            pltpu.SemaphoreType.DMA((len(parts), 3)),
            pltpu.SemaphoreType.DMA,
            pltpu.SemaphoreType.DMA((levels,)),
        ],
        compiler_params=large,
        name="local_sums",
    )(count, *hbm)
    k_sums = call(
        side_kernel,
        "side_sums",
        shape(wide, col_count),
        count,
        w_vmem,
        u_vmem,
        params=large,
        cost=6 * wide * row_count * col_count,
    )

    def lowest(solve, solve_send):
        if pair:
            return solve, swapped(solve_send, 0)
        solve = solve + swapped(solve_send, 0)
        for bit in range(1, base_bits):
            solve = solve + swapped(solve, bit)
        return solve, swapped(solve, base_bits)

    solve, sib_solve = lowest(solve, solve_send)
    own_solve = solve
    solves, zs, fresh = [], [], {}
    for k in range(levels):
        if k > 0:
            sib_solve = swapped(solve, base_bits + k)
        solves.append(sib_solve)
        placed = []
        if k == 1:
            top_got = swapped(fresh[top], base_bits + top)
            sent = fresh[top - 1]
            got = swapped(sent, base_bits + top - 1)
        elif 1 < k < top:
            bit = top - k
            sent = call(
                functools.partial(side_join_kernel, n_side[bit + 1]),
                f"side_join_{bit}",
                shape(sum(n_side[bit:]), half),
                fresh[bit],
                sent,
                got,
                zs[-1],
                *([top_got] if k == 2 else []),
                cost=2 * 10**10,
            )
            got = swapped(sent, base_bits + bit)
            placed = [sent]
        elif k == top:
            top_sum = call(side_top_kernel, "side_top", shape(n_side[top], half), sent, got, zs[-1])
            top_got = swapped(top_sum, base_bits + top - 1)
            placed = [top_sum]
        out_shape = [shape(order, half)]
        if k < top:
            out_shape.append(shape(sum(solve_rows(i, levels, rank) for i in range(k + 1, levels)), half))
        outs = call(
            functools.partial(level_kernel, (levels, rank, base_bits, len(placed)), k),
            f"level_{k}",
            out_shape,
            solve,
            sib_solve,
            nodes,
            *placed,
            cost=2 * 10**10,
        )
        zs.append(outs[0])
        if k < top:
            solve = outs[1]
        if k == 0:
            side, side_send = call(
                functools.partial(side_state_kernel, (levels, rank)),
                "side_state",
                [shape(sum(n_side), half)] * 2,
                k_sums,
                products,
                outs[0],
            )
            side, sib_side = lowest(side, side_send)
            first = call(
                functools.partial(side_first_kernel, n_side[0]),
                "side_first",
                [shape(size, half) for size in n_side[1:]],
                side,
                sib_side,
                outs[0],
            )
            fresh = dict(enumerate(first, 1))

    dims = (levels, rank, 1.0 / col_count**0.5)
    copies = 2 if pair else 1
    *low_other, low_own = call(
        functools.partial(end_low_kernel, dims, pair),
        "end_low",
        [shape(wide + low, half)] * copies,
        *zs,
        sib_side,
        sent,
        got,
        side,
    )
    low_other = swapped(low_other[0] if pair else low_own, 0)
    *top_other, top_own = call(
        functools.partial(end_kernel, dims, pair),
        "end_factors",
        [shape(wide + rank, half)] * copies,
        *solves,
        *zs,
        sib_side,
        sent,
        got,
        top_sum,
        top_got,
        own_solve,
        side,
        scratch=[pltpu.VMEM((sum(n_side[1:top]), half), F32), pltpu.VMEM((n_side[top], half), F32)],
        cost=2 * 10**10,
    )
    top_other = swapped(top_other[0] if pair else top_own, 0)

    sol_vmem = call(
        functools.partial(solution_kernel, (wide, chunk)),
        "solution_rows",
        shape(row_count, col_count),
        count,
        low_own,
        low_other,
        x_vmem,
        q_vmem,
        params=large,
        cost=2 * 10**9,
    )
    grad = shape(wide, row_count, dtype=jnp.bfloat16)
    sol, left, right = call(
        functools.partial(factor_kernel, (wide, chunk)),
        "factor_rows",
        [shape(row_count, col_count), grad, grad],
        count,
        low_own,
        low_other,
        top_own,
        top_other,
        sol_vmem,
        w_vmem,
        out_specs=[anywhere] * 3,
        scratch=[pltpu.VMEM(grad.shape, grad.dtype)] * 2 + [pltpu.SemaphoreType.DMA((2 * steps + 1,))],
        params=large,
    )
    return sol, left.reshape(coeff_basis.shape), right.reshape(coeff_basis.shape)


def solution(mesh):
    in_specs = (
        P(("groups", "leaf"), None),
        P(("groups", "leaf"), None),
        P(None, None, ("groups", "leaf")),
        P(None, None, ("groups", "leaf")),
        P("groups", None, None),
        P(("groups", "leaf")),
    )
    out_specs = (
        P(("groups", "leaf"), None),
        P(None, None, ("groups", "leaf")),
        P(None, None, ("groups", "leaf")),
    )
    return jax.shard_map(body, mesh=mesh, in_specs=in_specs, out_specs=out_specs, check_vma=False)
```

```python
import functools

import jax
import jax.numpy as jnp
from jax import lax
from jax.experimental import pallas as pl
from jax.experimental.pallas import tpu as pltpu
from jax.sharding import PartitionSpec as P


HIGH = lax.Precision.HIGH
F32 = jnp.float32
MIB = 2**20


def dot(a, b, dims=((1,), (0,))):
    return lax.dot_general(a, b, (dims, ((), ())), precision=HIGH, preferred_element_type=F32)


def pack(blocks):
    rows = []
    for i in range(0, len(blocks) - 1, 2):
        rows.append(jnp.concatenate([blocks[i], blocks[i + 1]], 1))
    if len(blocks) % 2:
        half = blocks[-1].shape[0] // 2
        rows.append(jnp.concatenate([blocks[-1][:half], blocks[-1][half:]], 1))
    return rows


def pack_rows(count, rank):
    return count // 2 * rank + count % 2 * (rank // 2)


def unpack(ref, start, count, rank):
    blocks = []
    for i in range(count):
        if i == count - 1 and count % 2:
            half = ref[start : start + rank // 2, :]
            blocks.append(jnp.concatenate([half[:, :rank], half[:, rank:]], 0))
        else:
            lane = i % 2 * rank
            blocks.append(ref[start : start + rank, lane : lane + rank])
            start += i % 2 * rank
    return blocks


def side_rows(level, levels, rank):
    return rank + pack_rows(levels - level, rank)


def solve_rows(level, levels, rank):
    return rank + pack_rows(levels - 1 - level, rank)


def holds_first():
    return lax.axis_index("leaf") % 2 == 0


def half_lanes(own, half):
    lane = jnp.where(holds_first(), 0 if own else half, half if own else 0)
    return pl.ds(pl.multiple_of(lane, half), half)


def row_parts(row_count):
    eighth = row_count // 8
    if eighth % 128:
        return [(0, row_count)]
    sizes = [eighth, 2 * eighth, 2 * eighth, 2 * eighth, eighth]
    return [(sum(sizes[:n]), size) for n, size in enumerate(sizes)]


def write_state(keep, send, acc, rank, blocks_of):
    half = acc.shape[1] // 2
    is_first = holds_first()
    at = 0
    for k in range(acc.shape[0] // rank):
        low = acc[k * rank : (k + 1) * rank, :half]
        high = acc[k * rank : (k + 1) * rank, half:]
        keep[at : at + rank, :] = jnp.where(is_first, low, high)
        send[at : at + rank, :] = jnp.where(is_first, high, low)
        at += rank
        for rows in pack(blocks_of(k)):
            keep[at : at + rows.shape[0], :] = rows
            send[at : at + rows.shape[0], :] = rows
            at += rows.shape[0]


def local_kernel(dims, parts, ahead, count_ref, x_hbm, w_hbm, u_hbm, q_hbm, node_ref, *refs):
    levels, rank, base_bits = dims
    keep, send, g_ref, nodes_out, x_all, w_all, u_all, q_all, c_acc, sems, w_sem, node_sems = refs
    position = lax.axis_index("leaf")

    def copies(n):
        part = pl.ds(*parts[n])
        pairs = [(u_hbm.at[:, part], u_all.at[:, part]), (x_hbm.at[part], x_all.at[part])]
        pairs.append((q_hbm.at[:, part], q_all.at[:, part]))
        return [pltpu.make_async_copy(a, b, sems.at[n, i]) for i, (a, b) in enumerate(pairs)]

    def node_copy(k):
        index = 2**levels - 2 ** (levels - k) + jnp.right_shift(position, base_bits + k + 1)
        return pltpu.make_async_copy(node_ref.at[index], nodes_out.at[k], node_sems.at[k])

    w_copy = pltpu.make_async_copy(w_hbm, w_all, w_sem)
    for n in range(ahead):
        for copy in copies(n):
            copy.start()
    for k in range(levels):
        node_copy(k).start()

    for n, (first, size) in enumerate(parts):
        @pl.when(position >= 0)
        def _():
            if n + ahead < len(parts):
                for copy in copies(n + ahead):
                    copy.start()
            if n + ahead == len(parts):
                w_copy.start()
            for copy in copies(n):
                copy.wait()
            part = pl.ds(first, size)
            place = first + lax.broadcasted_iota(jnp.int32, (1, size), 1)
            u = jnp.where(place < count_ref[:1, :1], u_all[:, part], 0.0)
            c = dot(u, x_all[part, :])
            g = dot(u, q_all[:, part], ((1,), (1,)))
            c_acc[...] = c if n == 0 else c_acc[...] + c
            g_ref[...] = g if n == 0 else g_ref[...] + g

    def blocks(k):
        lane = slice(k * rank, (k + 1) * rank)
        return [g_ref[i * rank : (i + 1) * rank, lane] for i in range(k + 1, levels)]

    write_state(keep, send, c_acc, rank, blocks)
    for k in range(levels):
        node_copy(k).wait()
    w_copy.wait()


def side_kernel(count_ref, w_ref, u_ref, k_ref):
    place = lax.broadcasted_iota(jnp.int32, (1, u_ref.shape[1]), 1)
    k_ref[...] = dot(jnp.where(place < count_ref[:1, :1], u_ref[...], 0.0), w_ref[...])


def side_state_kernel(dims, k_ref, g_ref, after_ref, keep, send):
    del after_ref
    levels, rank = dims

    def blocks(k):
        row = slice(k * rank, (k + 1) * rank)
        return [g_ref[row, j * rank : (j + 1) * rank] for j in range(k, levels)]

    write_state(keep, send, k_ref, rank, blocks)


def side_first_kernel(at, own_ref, sib_ref, after_ref, *out_refs):
    del after_ref
    for out_ref in out_refs:
        rows = out_ref.shape[0]
        out_ref[...] = own_ref[at : at + rows, :] + sib_ref[at : at + rows, :]
        at += rows


def side_join_kernel(first, fresh_ref, sent_ref, got_ref, after_ref, *refs):
    del after_ref
    *top_ref, out_ref = refs
    at, rows = fresh_ref.shape[0], got_ref.shape[0]
    out_ref[:at, :] = fresh_ref[...]
    out_ref[at : at + first, :] = got_ref[:first, :]
    if first < rows:
        out_ref[at + first : at + rows, :] = sent_ref[first:, :] + got_ref[first:, :]
    if top_ref:
        out_ref[at + rows :, :] = top_ref[0][...]


def side_top_kernel(sent_ref, got_ref, after_ref, out_ref):
    del after_ref
    at = sent_ref.shape[0] - out_ref.shape[0]
    out_ref[...] = sent_ref[at:, :] + got_ref[at:, :]


def level_kernel(dims, level, own_ref, sib_ref, nodes_ref, *refs):
    levels, rank, base_bits, placed = dims
    z_ref, *out_refs = refs[placed:]
    is_lower = jnp.right_shift(lax.axis_index("leaf"), base_bits + level) % 2 == 0
    own, sib = own_ref[:rank, :], sib_ref[:rank, :]
    both = jnp.concatenate([jnp.where(is_lower, own, sib), jnp.where(is_lower, sib, own)], 0)
    mixed = dot(nodes_ref[level], both)
    z_own = jnp.where(is_lower, mixed[:rank], mixed[rank:])
    z_sib = jnp.where(is_lower, mixed[rank:], mixed[:rank])
    z_ref[:rank, :] = z_own
    z_ref[rank:, :] = z_sib
    if not out_refs:
        return
    (out_ref,) = out_refs
    count = levels - 1 - level
    h_own = unpack(own_ref, rank, count, rank)
    h_sib = unpack(sib_ref, rank, count, rank)
    h_both = jnp.concatenate([jnp.concatenate(h_own, 0), jnp.concatenate(h_sib, 0)], 1)
    drop = dot(h_both, jnp.concatenate([z_own, z_sib], 0))

    def total(at, rows):
        return own_ref[at : at + rows, :] + sib_ref[at : at + rows, :]

    start = solve_rows(level, levels, rank)
    at = 0
    for i in range(count):
        out_ref[at : at + rank, :] = total(start + at, rank) - drop[i * rank : (i + 1) * rank]
        at += rank
        rest = solve_rows(level + 1 + i, levels, rank) - rank
        if rest:
            out_ref[at : at + rest, :] = total(start + at, rest)
            at += rest


def factor_terms(dims, k, c, side_ref, at, z_here, z_above):
    levels, rank, scale = dims
    blocks = unpack(side_ref, at + rank, levels - k, rank)
    z_here = jnp.concatenate([z_here, *z_above], 0)
    l_term = c - dot(jnp.concatenate(blocks, 1), z_here)
    return l_term * scale, side_ref[at : at + rank, :] * scale


def end_low_kernel(dims, pair, *refs):
    levels, rank, _ = dims
    solves, z_refs = refs[: levels - 1], refs[levels - 1 : 2 * levels - 1]
    sib_side, side_sent, side_got, own_solve, own_side = refs[2 * levels - 1 : 2 * levels + 4]
    *out_refs, side_sum = refs[2 * levels + 4 :]
    z_own = [z_ref[:rank, :] for z_ref in z_refs]

    low, rows = side_rows(1, levels, rank), side_sum.shape[0]
    side_sum[:low, :] = side_got[:low, :]
    side_sum[low:, :] = side_got[low:rows, :] + side_sent[low:rows, :]

    def write(out_ref, k, z_term, l_term, k_term):
        out_ref[k * rank : (k + 1) * rank, :] = z_term
        out_ref[(levels + k) * rank : (levels + k + 1) * rank, :] = l_term
        out_ref[(2 * levels - 1 + k) * rank : (2 * levels + k) * rank, :] = k_term

    at = 0
    for k in range(levels - 1):
        z_sib = z_refs[k][rank:, :]
        where = (sib_side, 0) if k == 0 else (side_sum, at)
        at += side_rows(k, levels, rank) if k > 0 else 0
        parts = (z_own[k], *factor_terms(dims, k, solves[k][:rank, :], *where, z_sib, z_own[k + 1 :]))
        write(out_refs[-1], k, *parts)
        if pair:
            if k == 0:
                parts = (z_sib, *factor_terms(dims, 0, own_solve[:rank, :], own_side, 0, z_own[0], z_own[1:]))
            write(out_refs[0], k, *parts)
    for out_ref in out_refs:
        out_ref[(levels - 1) * rank : levels * rank, :] = z_own[-1]


def end_top_kernel(dims, solve_ref, z_ref, sent_ref, got_ref, out_ref, side_ref):
    levels, rank, _ = dims
    side_ref[...] = sent_ref[...] + got_ref[...]
    l_term, k_term = factor_terms(dims, levels - 1, solve_ref[:rank, :], side_ref, 0, z_ref[rank:, :], [])
    out_ref[:rank, :] = l_term
    out_ref[rank:, :] = k_term


def whole(own_ref, other_ref, start, rows):
    is_first = holds_first()
    own, other = own_ref[start : start + rows, :], other_ref[start : start + rows, :]
    return jnp.concatenate([jnp.where(is_first, own, other), jnp.where(is_first, other, own)], 1)


class Sender:
    def __init__(self, sems):
        self.sems, self.copies = sems, []

    def send(self, source, target):
        copy = pltpu.make_async_copy(source, target, self.sems.at[len(self.copies)])
        copy.start()
        self.copies.append(copy)

    def wait(self):
        for copy in self.copies:
            copy.wait()


def halves(value):
    high = value.astype(jnp.bfloat16)
    return high, (value - high.astype(F32)).astype(jnp.bfloat16)


def solution_kernel(dims, count_ref, x_ref, q_ref, *refs):
    own, rank, chunk = dims
    *z_refs, sol = refs
    half = sol.shape[1]
    if own:
        z = jnp.concatenate([z_ref[:rank, :] for z_ref in z_refs], 0)
    else:
        z = z_refs[0][: q_ref.shape[0], :]
    z_high, z_low = halves(z)
    z_both = jnp.concatenate([z_high, z_low], 1)
    lanes = half_lanes(own, half)
    dims = (((0,), (0,)), ((), ()))
    for i in range(x_ref.shape[0] // chunk):
        part = slice(i * chunk, (i + 1) * chunk)
        live = i * chunk + lax.broadcasted_iota(jnp.int32, (chunk, 1), 0) < count_ref[:1, :1]
        q_high, q_low = halves(q_ref[:, part])
        both = lax.dot_general(q_high, z_both, dims, preferred_element_type=F32)
        rest = lax.dot_general(q_low, z_high, dims, preferred_element_type=F32)
        x = x_ref[part, lanes] - (both[:, :half] + (both[:, half:] + rest))
        sol[part, :] = jnp.where(live, x, 0.0)


def factor_kernel(dims, count_ref, low_own, low_other, top_own, top_other, x_own, x_other, w_ref, *refs):
    wide, chunk = dims
    sol_out, left_out, right_out, left, right, sems = refs
    sender = Sender(sems)
    half = x_own.shape[1]
    sender.send(x_own, sol_out.at[:, half_lanes(True, half)])
    sender.send(x_other, sol_out.at[:, half_lanes(False, half)])
    rank = top_own.shape[0] // 2
    low = wide - rank

    def joined(own_ref, other_ref, start, rows):
        return jnp.concatenate([own_ref[start : start + rows, :], other_ref[start : start + rows, :]], 1)

    l = jnp.concatenate([whole(low_own, low_other, wide, low), whole(top_own, top_other, 0, rank)], 0)
    k = jnp.concatenate([joined(low_own, low_other, wide + low, low), joined(top_own, top_other, rank, rank)], 0)
    for i in range(w_ref.shape[0] // chunk):
        part, place = slice(i * chunk, (i + 1) * chunk), pl.ds(i * chunk, chunk)
        live = i * chunk + lax.broadcasted_iota(jnp.int32, (1, chunk), 1) < count_ref[:1, :1]
        left_now = dot(l, w_ref[part, :], ((1,), (1,)))
        left[:, part] = jnp.where(live, left_now, 0.0).astype(left.dtype)
        sender.send(left.at[:, place], left_out.at[:, place])
        x = jnp.concatenate([x_own[part, :], x_other[part, :]], 1)
        right[:, part] = dot(k, x, ((1,), (1,))).astype(right.dtype)
        sender.send(right.at[:, place], right_out.at[:, place])
    sender.wait()


def swapped(value, bit):
    mask = 2**bit
    pairs = [(source, source ^ mask) for source in range(lax.axis_size("leaf"))]
    return lax.ppermute(value, "leaf", pairs)


def shape(*sizes, dtype=F32):
    return jax.ShapeDtypeStruct(sizes, dtype)


def body(right_side, cotangent, coeff_basis, saved_basis, node_inverse, leaf_rows):
    row_count, col_count = right_side.shape
    levels, rank = coeff_basis.shape[:2]
    wide, order, half = levels * rank, 2 * rank, col_count // 2
    low, top = wide - rank, levels - 1
    base_bits = lax.axis_size("leaf").bit_length() - 1 - levels
    pair = base_bits == 0
    chunk = min(512, row_count)
    steps = row_count // chunk
    parts = row_parts(row_count)
    u_all = coeff_basis.reshape(wide, row_count)
    q_all = saved_basis.reshape(wide, row_count)

    vmem = pl.BlockSpec(memory_space=pltpu.VMEM)
    anywhere = pl.BlockSpec(memory_space=pl.ANY)
    small = pltpu.CompilerParams(vmem_limit_bytes=4 * MIB)
    large = pltpu.CompilerParams(vmem_limit_bytes=20 * MIB)

    def call(kernel, name, out_shape, *operands, out_specs=vmem, scratch=(), params=small, cost=None, **options):
        if isinstance(out_shape, list) and out_specs is vmem:
            out_specs = [vmem] * len(out_shape)
        if cost is not None:
            options["cost_estimate"] = pl.CostEstimate(flops=cost, bytes_accessed=MIB, transcendentals=0)
        return pl.pallas_call(
            kernel,
            out_shape=out_shape,
            in_specs=[vmem] * len(operands),
            out_specs=out_specs,
            scratch_shapes=list(scratch),
            compiler_params=params,
            name=name,
            **options,
        )(*operands)

    n_solve = sum(solve_rows(k, levels, rank) for k in range(levels))
    n_side = [side_rows(k, levels, rank) for k in range(levels)]
    arrays = (right_side, cotangent, u_all, q_all)
    outs = [shape(n_solve, half), shape(n_solve, half), shape(wide, wide), shape(levels, order, order)]
    outs += [shape(*a.shape) for a in arrays]
    count = jnp.broadcast_to(leaf_rows[:, None], (8, 128))
    hbm = [pltpu.with_memory_space_constraint(a, pltpu.HBM) for a in (*arrays, node_inverse)]
    solve, solve_send, products, nodes, x_vmem, w_vmem, u_vmem, q_vmem = pl.pallas_call(
        functools.partial(local_kernel, (levels, rank, base_bits), parts, min(3, len(parts))),
        out_shape=outs,
        in_specs=[vmem] + [anywhere] * 5,
        out_specs=[vmem] * 8,
        scratch_shapes=[
            pltpu.VMEM((wide, col_count), F32),
            pltpu.SemaphoreType.DMA((len(parts), 3)),
            pltpu.SemaphoreType.DMA,
            pltpu.SemaphoreType.DMA((levels,)),
        ],
        compiler_params=large,
        name="local_sums",
    )(count, *hbm)
    k_sums = call(
        side_kernel,
        "side_sums",
        shape(wide, col_count),
        count,
        w_vmem,
        u_vmem,
        params=large,
        cost=6 * wide * row_count * col_count,
    )

    def lowest(solve, solve_send):
        if pair:
            return solve, swapped(solve_send, 0)
        solve = solve + swapped(solve_send, 0)
        for bit in range(1, base_bits):
            solve = solve + swapped(solve, bit)
        return solve, swapped(solve, base_bits)

    solve, sib_solve = lowest(solve, solve_send)
    own_solve = solve
    solves, zs, fresh = [], [], {}
    for k in range(levels):
        if k > 0:
            sib_solve = swapped(solve, base_bits + k)
        solves.append(sib_solve)
        placed = []
        if k == 1:
            top_got = swapped(fresh[top], base_bits + top)
            sent = fresh[top - 1]
            got = swapped(sent, base_bits + top - 1)
        elif 1 < k < top:
            bit = top - k
            sent = call(
                functools.partial(side_join_kernel, n_side[bit + 1]),
                f"side_join_{bit}",
                shape(sum(n_side[bit:]), half),
                fresh[bit],
                sent,
                got,
                zs[-1],
                *([top_got] if k == 2 else []),
                cost=2 * 10**10,
            )
            got = swapped(sent, base_bits + bit)
            placed = [sent]
        elif k == top:
            top_sum = call(side_top_kernel, "side_top", shape(n_side[top], half), sent, got, zs[-1])
            top_got = swapped(top_sum, base_bits + top - 1)
            placed = [top_sum]
        out_shape = [shape(order, half)]
        if k < top:
            out_shape.append(shape(sum(solve_rows(i, levels, rank) for i in range(k + 1, levels)), half))
        outs = call(
            functools.partial(level_kernel, (levels, rank, base_bits, len(placed)), k),
            f"level_{k}",
            out_shape,
            solve,
            sib_solve,
            nodes,
            *placed,
            cost=2 * 10**10,
        )
        zs.append(outs[0])
        if k < top:
            solve = outs[1]
        if k == 0:
            side, side_send = call(
                functools.partial(side_state_kernel, (levels, rank)),
                "side_state",
                [shape(sum(n_side), half)] * 2,
                k_sums,
                products,
                outs[0],
            )
            side, sib_side = lowest(side, side_send)
            first = call(
                functools.partial(side_first_kernel, n_side[0]),
                "side_first",
                [shape(size, half) for size in n_side[1:]],
                side,
                sib_side,
                outs[0],
            )
            fresh = dict(enumerate(first, 1))

    dims = (levels, rank, 1.0 / col_count**0.5)
    copies = 2 if pair else 1
    *low_other, low_own = call(
        functools.partial(end_low_kernel, dims, pair),
        "end_low",
        [shape(wide + 2 * low, half)] * copies,
        *solves[:top],
        *zs,
        sib_side,
        sent,
        got,
        own_solve,
        side,
        scratch=[pltpu.VMEM((sum(n_side[1:top]), half), F32)],
    )
    low_other = swapped(low_other[0] if pair else low_own, 0)
    top_own = call(
        functools.partial(end_top_kernel, dims),
        "end_top",
        shape(order, half),
        solves[top],
        zs[top],
        top_sum,
        top_got,
        scratch=[pltpu.VMEM((n_side[top], half), F32)],
        cost=2 * 10**10,
    )
    top_other = swapped(top_own, 0)

    sol_own = call(
        functools.partial(solution_kernel, (True, rank, chunk)),
        "solution_own",
        shape(row_count, half),
        count,
        x_vmem,
        q_vmem,
        *zs,
        params=large,
        cost=10**9,
    )
    sol_other = call(
        functools.partial(solution_kernel, (False, rank, chunk)),
        "solution_other",
        shape(row_count, half),
        count,
        x_vmem,
        q_vmem,
        low_other,
        params=large,
        cost=10**9,
    )
    grad = shape(wide, row_count, dtype=jnp.bfloat16)
    sol, left, right = call(
        functools.partial(factor_kernel, (wide, chunk)),
        "factor_rows",
        [shape(row_count, col_count), grad, grad],
        count,
        low_own,
        low_other,
        top_own,
        top_other,
        sol_own,
        sol_other,
        w_vmem,
        out_specs=[anywhere] * 3,
        scratch=[pltpu.VMEM(grad.shape, grad.dtype)] * 2 + [pltpu.SemaphoreType.DMA((2 * steps + 2,))],
        params=large,
    )
    return sol, left.reshape(coeff_basis.shape), right.reshape(coeff_basis.shape)


def solution(mesh):
    in_specs = (
        P(("groups", "leaf"), None),
        P(("groups", "leaf"), None),
        P(None, None, ("groups", "leaf")),
        P(None, None, ("groups", "leaf")),
        P("groups", None, None),
        P(("groups", "leaf")),
    )
    out_specs = (
        P(("groups", "leaf"), None),
        P(None, None, ("groups", "leaf")),
        P(None, None, ("groups", "leaf")),
    )
    return jax.shard_map(body, mesh=mesh, in_specs=in_specs, out_specs=out_specs, check_vma=False)
```

```python
import functools

import jax
import jax.numpy as jnp
from jax import lax
from jax.experimental import pallas as pl
from jax.experimental.pallas import tpu as pltpu
from jax.sharding import PartitionSpec as P


HIGH = lax.Precision.HIGH
F32 = jnp.float32
MIB = 2**20


def dot(a, b, dims=((1,), (0,))):
    return lax.dot_general(a, b, (dims, ((), ())), precision=HIGH, preferred_element_type=F32)


def pack(blocks):
    rows = []
    for i in range(0, len(blocks) - 1, 2):
        rows.append(jnp.concatenate([blocks[i], blocks[i + 1]], 1))
    if len(blocks) % 2:
        half = blocks[-1].shape[0] // 2
        rows.append(jnp.concatenate([blocks[-1][:half], blocks[-1][half:]], 1))
    return rows


def pack_rows(count, rank):
    return count // 2 * rank + count % 2 * (rank // 2)


def unpack(ref, start, count, rank):
    blocks = []
    for i in range(count):
        if i == count - 1 and count % 2:
            half = ref[start : start + rank // 2, :]
            blocks.append(jnp.concatenate([half[:, :rank], half[:, rank:]], 0))
        else:
            lane = i % 2 * rank
            blocks.append(ref[start : start + rank, lane : lane + rank])
            start += i % 2 * rank
    return blocks


def side_rows(level, levels, rank):
    return rank + pack_rows(levels - level, rank)


def solve_rows(level, levels, rank):
    return rank + pack_rows(levels - 1 - level, rank)


def holds_first():
    return lax.axis_index("leaf") % 2 == 0


def half_lanes(own, half):
    lane = jnp.where(holds_first(), 0 if own else half, half if own else 0)
    return pl.ds(pl.multiple_of(lane, half), half)


def row_parts(row_count):
    eighth = row_count // 8
    if eighth % 128:
        return [(0, row_count)]
    sizes = [eighth, 2 * eighth, 2 * eighth, 2 * eighth, eighth]
    return [(sum(sizes[:n]), size) for n, size in enumerate(sizes)]


def write_state(keep, send, acc, rank, blocks_of):
    half = acc.shape[1] // 2
    is_first = holds_first()
    at = 0
    for k in range(acc.shape[0] // rank):
        low = acc[k * rank : (k + 1) * rank, :half]
        high = acc[k * rank : (k + 1) * rank, half:]
        keep[at : at + rank, :] = jnp.where(is_first, low, high)
        send[at : at + rank, :] = jnp.where(is_first, high, low)
        at += rank
        for rows in pack(blocks_of(k)):
            keep[at : at + rows.shape[0], :] = rows
            send[at : at + rows.shape[0], :] = rows
            at += rows.shape[0]


def local_kernel(dims, parts, ahead, count_ref, x_hbm, w_hbm, u_hbm, q_hbm, node_ref, *refs):
    levels, rank, base_bits = dims
    keep, send, g_ref, nodes_out, x_all, w_all, u_all, q_all, c_acc, sems, w_sem, node_sems = refs
    position = lax.axis_index("leaf")

    def copies(n):
        part = pl.ds(*parts[n])
        pairs = [(u_hbm.at[:, part], u_all.at[:, part]), (x_hbm.at[part], x_all.at[part])]
        pairs.append((q_hbm.at[:, part], q_all.at[:, part]))
        return [pltpu.make_async_copy(a, b, sems.at[n, i]) for i, (a, b) in enumerate(pairs)]

    def node_copy(k):
        index = 2**levels - 2 ** (levels - k) + jnp.right_shift(position, base_bits + k + 1)
        return pltpu.make_async_copy(node_ref.at[index], nodes_out.at[k], node_sems.at[k])

    w_copy = pltpu.make_async_copy(w_hbm, w_all, w_sem)
    for n in range(ahead):
        for copy in copies(n):
            copy.start()
    for k in range(levels):
        node_copy(k).start()

    for n, (first, size) in enumerate(parts):
        @pl.when(position >= 0)
        def _():
            if n + ahead < len(parts):
                for copy in copies(n + ahead):
                    copy.start()
            if n + ahead == len(parts):
                w_copy.start()
            for copy in copies(n):
                copy.wait()
            part = pl.ds(first, size)
            place = first + lax.broadcasted_iota(jnp.int32, (1, size), 1)
            u = jnp.where(place < count_ref[:1, :1], u_all[:, part], 0.0)
            c = dot(u, x_all[part, :])
            g = dot(u, q_all[:, part], ((1,), (1,)))
            c_acc[...] = c if n == 0 else c_acc[...] + c
            g_ref[...] = g if n == 0 else g_ref[...] + g

    def blocks(k):
        lane = slice(k * rank, (k + 1) * rank)
        return [g_ref[i * rank : (i + 1) * rank, lane] for i in range(k + 1, levels)]

    write_state(keep, send, c_acc, rank, blocks)
    for k in range(levels):
        node_copy(k).wait()
    w_copy.wait()


def side_kernel(count_ref, w_ref, u_ref, k_ref):
    place = lax.broadcasted_iota(jnp.int32, (1, u_ref.shape[1]), 1)
    k_ref[...] = dot(jnp.where(place < count_ref[:1, :1], u_ref[...], 0.0), w_ref[...])


def side_state_kernel(dims, k_ref, g_ref, after_ref, keep, send):
    del after_ref
    levels, rank = dims

    def blocks(k):
        row = slice(k * rank, (k + 1) * rank)
        return [g_ref[row, j * rank : (j + 1) * rank] for j in range(k, levels)]

    write_state(keep, send, k_ref, rank, blocks)


def side_first_kernel(at, own_ref, sib_ref, after_ref, *out_refs):
    del after_ref
    for out_ref in out_refs:
        rows = out_ref.shape[0]
        out_ref[...] = own_ref[at : at + rows, :] + sib_ref[at : at + rows, :]
        at += rows


def side_join_kernel(first, fresh_ref, sent_ref, got_ref, after_ref, *refs):
    del after_ref
    *top_ref, out_ref = refs
    at, rows = fresh_ref.shape[0], got_ref.shape[0]
    out_ref[:at, :] = fresh_ref[...]
    out_ref[at : at + first, :] = got_ref[:first, :]
    if first < rows:
        out_ref[at + first : at + rows, :] = sent_ref[first:, :] + got_ref[first:, :]
    if top_ref:
        out_ref[at + rows :, :] = top_ref[0][...]


def side_top_kernel(sent_ref, got_ref, after_ref, out_ref):
    del after_ref
    at = sent_ref.shape[0] - out_ref.shape[0]
    out_ref[...] = sent_ref[at:, :] + got_ref[at:, :]


def level_kernel(dims, level, own_ref, sib_ref, nodes_ref, *refs):
    levels, rank, base_bits, placed = dims
    z_ref, *out_refs = refs[placed:]
    is_lower = jnp.right_shift(lax.axis_index("leaf"), base_bits + level) % 2 == 0
    own, sib = own_ref[:rank, :], sib_ref[:rank, :]
    both = jnp.concatenate([jnp.where(is_lower, own, sib), jnp.where(is_lower, sib, own)], 0)
    mixed = dot(nodes_ref[level], both)
    z_own = jnp.where(is_lower, mixed[:rank], mixed[rank:])
    z_sib = jnp.where(is_lower, mixed[rank:], mixed[:rank])
    z_ref[:rank, :] = z_own
    z_ref[rank:, :] = z_sib
    if not out_refs:
        return
    (out_ref,) = out_refs
    count = levels - 1 - level
    h_own = unpack(own_ref, rank, count, rank)
    h_sib = unpack(sib_ref, rank, count, rank)
    h_both = jnp.concatenate([jnp.concatenate(h_own, 0), jnp.concatenate(h_sib, 0)], 1)
    drop = dot(h_both, jnp.concatenate([z_own, z_sib], 0))

    def total(at, rows):
        return own_ref[at : at + rows, :] + sib_ref[at : at + rows, :]

    start = solve_rows(level, levels, rank)
    at = 0
    for i in range(count):
        out_ref[at : at + rank, :] = total(start + at, rank) - drop[i * rank : (i + 1) * rank]
        at += rank
        rest = solve_rows(level + 1 + i, levels, rank) - rank
        if rest:
            out_ref[at : at + rest, :] = total(start + at, rest)
            at += rest


def factor_terms(dims, k, c, side_ref, at, z_here, z_above):
    levels, rank, scale = dims
    blocks = unpack(side_ref, at + rank, levels - k, rank)
    z_here = jnp.concatenate([z_here, *z_above], 0)
    l_term = c - dot(jnp.concatenate(blocks, 1), z_here)
    return l_term * scale, side_ref[at : at + rank, :] * scale


def end_low_kernel(dims, pair, *refs):
    levels, rank, _ = dims
    solves, z_refs = refs[:levels], refs[levels : 2 * levels]
    sib_side, side_sent, side_got, own_solve, own_side = refs[2 * levels : 2 * levels + 5]
    *out_refs, side_sum = refs[2 * levels + 5 :]
    z_own = [z_ref[:rank, :] for z_ref in z_refs]

    low, rows = side_rows(1, levels, rank), side_sum.shape[0]
    side_sum[:low, :] = side_got[:low, :]
    side_sum[low:, :] = side_got[low:rows, :] + side_sent[low:rows, :]

    def write(out_ref, k, z_term, l_term, k_term):
        out_ref[k * rank : (k + 1) * rank, :] = z_term
        out_ref[(levels + k) * rank : (levels + k + 1) * rank, :] = l_term
        out_ref[(2 * levels - 1 + k) * rank : (2 * levels + k) * rank, :] = k_term

    at = 0
    for k in range(levels - 1):
        z_sib = z_refs[k][rank:, :]
        where = (sib_side, 0) if k == 0 else (side_sum, at)
        at += side_rows(k, levels, rank) if k > 0 else 0
        parts = (z_own[k], *factor_terms(dims, k, solves[k][:rank, :], *where, z_sib, z_own[k + 1 :]))
        write(out_refs[-1], k, *parts)
        if pair:
            if k == 0:
                parts = (z_sib, *factor_terms(dims, 0, own_solve[:rank, :], own_side, 0, z_own[0], z_own[1:]))
            write(out_refs[0], k, *parts)
    for out_ref in out_refs:
        out_ref[(levels - 1) * rank : levels * rank, :] = z_own[-1]
        out_ref[(3 * levels - 2) * rank : (3 * levels - 1) * rank, :] = solves[-1][:rank, :]
        out_ref[(3 * levels - 1) * rank :, :] = z_refs[-1][rank:, :]


def end_top_kernel(sent_ref, got_ref, k_ref, h_ref):
    rank = k_ref.shape[0]
    k_ref[...] = sent_ref[:rank, :] + got_ref[:rank, :]
    h_ref[...] = sent_ref[rank:, :] + got_ref[rank:, :]


def whole(own_ref, other_ref, start, rows):
    is_first = holds_first()
    own, other = own_ref[start : start + rows, :], other_ref[start : start + rows, :]
    return jnp.concatenate([jnp.where(is_first, own, other), jnp.where(is_first, other, own)], 1)


class Sender:
    def __init__(self, sems):
        self.sems, self.copies = sems, []

    def send(self, source, target):
        copy = pltpu.make_async_copy(source, target, self.sems.at[len(self.copies)])
        copy.start()
        self.copies.append(copy)

    def wait(self):
        for copy in self.copies:
            copy.wait()


def halves(value):
    high = value.astype(jnp.bfloat16)
    return high, (value - high.astype(F32)).astype(jnp.bfloat16)


def solution_kernel(dims, count_ref, x_ref, q_ref, *refs):
    own, rank, chunk = dims
    *z_refs, sol = refs
    half = sol.shape[1]
    if own:
        z = jnp.concatenate([z_ref[:rank, :] for z_ref in z_refs], 0)
    else:
        z = z_refs[0][: q_ref.shape[0], :]
    z_high, z_low = halves(z)
    z_both = jnp.concatenate([z_high, z_low], 1)
    lanes = half_lanes(own, half)
    dims = (((0,), (0,)), ((), ()))
    for i in range(x_ref.shape[0] // chunk):
        part = slice(i * chunk, (i + 1) * chunk)
        live = i * chunk + lax.broadcasted_iota(jnp.int32, (chunk, 1), 0) < count_ref[:1, :1]
        q_high, q_low = halves(q_ref[:, part])
        both = lax.dot_general(q_high, z_both, dims, preferred_element_type=F32)
        rest = lax.dot_general(q_low, z_high, dims, preferred_element_type=F32)
        x = x_ref[part, lanes] - (both[:, :half] + (both[:, half:] + rest))
        sol[part, :] = jnp.where(live, x, 0.0)


def factor_kernel(dims, count_ref, low_own, low_other, k_own, k_other, h_ref, x_own, x_other, w_ref, *refs):
    wide, scale, chunk = dims
    sol_out, left_out, right_out, left, right, sems = refs
    sender = Sender(sems)
    half = x_own.shape[1]
    sender.send(x_own, sol_out.at[:, half_lanes(True, half)])
    sender.send(x_other, sol_out.at[:, half_lanes(False, half)])
    rank = k_own.shape[0]
    low = wide - rank
    at = wide + 2 * low
    (block,) = unpack(h_ref, 0, 1, rank)
    l_top = whole(low_own, low_other, at, rank) - dot(block, whole(low_own, low_other, at + rank, rank))
    l = jnp.concatenate([whole(low_own, low_other, wide, low), l_top * scale], 0)
    k_low = jnp.concatenate([low_own[wide + low : at, :], low_other[wide + low : at, :]], 1)
    k = jnp.concatenate([k_low, jnp.concatenate([k_own[...], k_other[...]], 1) * scale], 0)
    for i in range(w_ref.shape[0] // chunk):
        part, place = slice(i * chunk, (i + 1) * chunk), pl.ds(i * chunk, chunk)
        live = i * chunk + lax.broadcasted_iota(jnp.int32, (1, chunk), 1) < count_ref[:1, :1]
        left_now = dot(l, w_ref[part, :], ((1,), (1,)))
        left[:, part] = jnp.where(live, left_now, 0.0).astype(left.dtype)
        sender.send(left.at[:, place], left_out.at[:, place])
        x = jnp.concatenate([x_own[part, :], x_other[part, :]], 1)
        right[:, part] = dot(k, x, ((1,), (1,))).astype(right.dtype)
        sender.send(right.at[:, place], right_out.at[:, place])
    sender.wait()


def swapped(value, bit):
    mask = 2**bit
    pairs = [(source, source ^ mask) for source in range(lax.axis_size("leaf"))]
    return lax.ppermute(value, "leaf", pairs)


def shape(*sizes, dtype=F32):
    return jax.ShapeDtypeStruct(sizes, dtype)


def body(right_side, cotangent, coeff_basis, saved_basis, node_inverse, leaf_rows):
    row_count, col_count = right_side.shape
    levels, rank = coeff_basis.shape[:2]
    wide, order, half = levels * rank, 2 * rank, col_count // 2
    low, top = wide - rank, levels - 1
    base_bits = lax.axis_size("leaf").bit_length() - 1 - levels
    pair = base_bits == 0
    chunk = min(512, row_count)
    steps = row_count // chunk
    parts = row_parts(row_count)
    u_all = coeff_basis.reshape(wide, row_count)
    q_all = saved_basis.reshape(wide, row_count)

    vmem = pl.BlockSpec(memory_space=pltpu.VMEM)
    anywhere = pl.BlockSpec(memory_space=pl.ANY)
    small = pltpu.CompilerParams(vmem_limit_bytes=4 * MIB)
    large = pltpu.CompilerParams(vmem_limit_bytes=20 * MIB)

    def call(kernel, name, out_shape, *operands, out_specs=vmem, scratch=(), params=small, cost=None, **options):
        if isinstance(out_shape, list) and out_specs is vmem:
            out_specs = [vmem] * len(out_shape)
        if cost is not None:
            options["cost_estimate"] = pl.CostEstimate(flops=cost, bytes_accessed=MIB, transcendentals=0)
        return pl.pallas_call(
            kernel,
            out_shape=out_shape,
            in_specs=[vmem] * len(operands),
            out_specs=out_specs,
            scratch_shapes=list(scratch),
            compiler_params=params,
            name=name,
            **options,
        )(*operands)

    n_solve = sum(solve_rows(k, levels, rank) for k in range(levels))
    n_side = [side_rows(k, levels, rank) for k in range(levels)]
    arrays = (right_side, cotangent, u_all, q_all)
    outs = [shape(n_solve, half), shape(n_solve, half), shape(wide, wide), shape(levels, order, order)]
    outs += [shape(*a.shape) for a in arrays]
    count = jnp.broadcast_to(leaf_rows[:, None], (8, 128))
    hbm = [pltpu.with_memory_space_constraint(a, pltpu.HBM) for a in (*arrays, node_inverse)]
    solve, solve_send, products, nodes, x_vmem, w_vmem, u_vmem, q_vmem = pl.pallas_call(
        functools.partial(local_kernel, (levels, rank, base_bits), parts, min(3, len(parts))),
        out_shape=outs,
        in_specs=[vmem] + [anywhere] * 5,
        out_specs=[vmem] * 8,
        scratch_shapes=[
            pltpu.VMEM((wide, col_count), F32),
            pltpu.SemaphoreType.DMA((len(parts), 3)),
            pltpu.SemaphoreType.DMA,
            pltpu.SemaphoreType.DMA((levels,)),
        ],
        compiler_params=large,
        name="local_sums",
    )(count, *hbm)
    k_sums = call(
        side_kernel,
        "side_sums",
        shape(wide, col_count),
        count,
        w_vmem,
        u_vmem,
        params=large,
        cost=6 * wide * row_count * col_count,
    )

    def lowest(solve, solve_send):
        if pair:
            return solve, swapped(solve_send, 0)
        solve = solve + swapped(solve_send, 0)
        for bit in range(1, base_bits):
            solve = solve + swapped(solve, bit)
        return solve, swapped(solve, base_bits)

    solve, sib_solve = lowest(solve, solve_send)
    own_solve = solve
    solves, zs, fresh = [], [], {}
    for k in range(levels):
        if k > 0:
            sib_solve = swapped(solve, base_bits + k)
        solves.append(sib_solve)
        placed = []
        if k == 1:
            top_got = swapped(fresh[top], base_bits + top)
            sent = fresh[top - 1]
            got = swapped(sent, base_bits + top - 1)
        elif 1 < k < top:
            bit = top - k
            sent = call(
                functools.partial(side_join_kernel, n_side[bit + 1]),
                f"side_join_{bit}",
                shape(sum(n_side[bit:]), half),
                fresh[bit],
                sent,
                got,
                zs[-1],
                *([top_got] if k == 2 else []),
                cost=2 * 10**10,
            )
            got = swapped(sent, base_bits + bit)
            placed = [sent]
        elif k == top:
            top_sum = call(side_top_kernel, "side_top", shape(n_side[top], half), sent, got, zs[-1])
            top_got = swapped(top_sum, base_bits + top - 1)
            placed = [top_sum]
        out_shape = [shape(order, half)]
        if k < top:
            out_shape.append(shape(sum(solve_rows(i, levels, rank) for i in range(k + 1, levels)), half))
        outs = call(
            functools.partial(level_kernel, (levels, rank, base_bits, len(placed)), k),
            f"level_{k}",
            out_shape,
            solve,
            sib_solve,
            nodes,
            *placed,
            cost=2 * 10**10,
        )
        zs.append(outs[0])
        if k < top:
            solve = outs[1]
        if k == 0:
            side, side_send = call(
                functools.partial(side_state_kernel, (levels, rank)),
                "side_state",
                [shape(sum(n_side), half)] * 2,
                k_sums,
                products,
                outs[0],
            )
            side, sib_side = lowest(side, side_send)
            first = call(
                functools.partial(side_first_kernel, n_side[0]),
                "side_first",
                [shape(size, half) for size in n_side[1:]],
                side,
                sib_side,
                outs[0],
            )
            fresh = dict(enumerate(first, 1))

    dims = (levels, rank, 1.0 / col_count**0.5)
    copies = 2 if pair else 1
    *low_other, low_own = call(
        functools.partial(end_low_kernel, dims, pair),
        "end_low",
        [shape(wide + 2 * low + order, half)] * copies,
        *solves,
        *zs,
        sib_side,
        sent,
        got,
        own_solve,
        side,
        scratch=[pltpu.VMEM((sum(n_side[1:top]), half), F32)],
    )
    low_other = swapped(low_other[0] if pair else low_own, 0)
    k_own, h_top = call(
        end_top_kernel,
        "end_top",
        [shape(rank, half), shape(n_side[top] - rank, half)],
        top_sum,
        top_got,
        cost=2 * 10**10,
    )
    k_other = swapped(k_own, 0)

    sol_own = call(
        functools.partial(solution_kernel, (True, rank, chunk)),
        "solution_own",
        shape(row_count, half),
        count,
        x_vmem,
        q_vmem,
        *zs,
        params=large,
        cost=10**9,
    )
    sol_other = call(
        functools.partial(solution_kernel, (False, rank, chunk)),
        "solution_other",
        shape(row_count, half),
        count,
        x_vmem,
        q_vmem,
        low_other,
        params=large,
        cost=10**9,
    )
    grad = shape(wide, row_count, dtype=jnp.bfloat16)
    sol, left, right = call(
        functools.partial(factor_kernel, (wide, dims[2], chunk)),
        "factor_rows",
        [shape(row_count, col_count), grad, grad],
        count,
        low_own,
        low_other,
        k_own,
        k_other,
        h_top,
        sol_own,
        sol_other,
        w_vmem,
        out_specs=[anywhere] * 3,
        scratch=[pltpu.VMEM(grad.shape, grad.dtype)] * 2 + [pltpu.SemaphoreType.DMA((2 * steps + 2,))],
        params=large,
    )
    return sol, left.reshape(coeff_basis.shape), right.reshape(coeff_basis.shape)


def solution(mesh):
    in_specs = (
        P(("groups", "leaf"), None),
        P(("groups", "leaf"), None),
        P(None, None, ("groups", "leaf")),
        P(None, None, ("groups", "leaf")),
        P("groups", None, None),
        P(("groups", "leaf")),
    )
    out_specs = (
        P(("groups", "leaf"), None),
        P(None, None, ("groups", "leaf")),
        P(None, None, ("groups", "leaf")),
    )
    return jax.shard_map(body, mesh=mesh, in_specs=in_specs, out_specs=out_specs, check_vma=False)
```

```python
import functools

import jax
import jax.numpy as jnp
from jax import lax
from jax.experimental import pallas as pl
from jax.experimental.pallas import tpu as pltpu
from jax.sharding import PartitionSpec as P


HIGH = lax.Precision.HIGH
F32 = jnp.float32
MIB = 2**20


def dot(a, b, dims=((1,), (0,))):
    return lax.dot_general(a, b, (dims, ((), ())), precision=HIGH, preferred_element_type=F32)


def pack(blocks):
    rows = []
    for i in range(0, len(blocks) - 1, 2):
        rows.append(jnp.concatenate([blocks[i], blocks[i + 1]], 1))
    if len(blocks) % 2:
        half = blocks[-1].shape[0] // 2
        rows.append(jnp.concatenate([blocks[-1][:half], blocks[-1][half:]], 1))
    return rows


def pack_rows(count, rank):
    return count // 2 * rank + count % 2 * (rank // 2)


def unpack(ref, start, count, rank):
    blocks = []
    for i in range(count):
        if i == count - 1 and count % 2:
            half = ref[start : start + rank // 2, :]
            blocks.append(jnp.concatenate([half[:, :rank], half[:, rank:]], 0))
        else:
            lane = i % 2 * rank
            blocks.append(ref[start : start + rank, lane : lane + rank])
            start += i % 2 * rank
    return blocks


def side_rows(level, levels, rank):
    return rank + pack_rows(levels - level, rank)


def solve_rows(level, levels, rank):
    return rank + pack_rows(levels - 1 - level, rank)


def holds_first():
    return lax.axis_index("leaf") % 2 == 0


def half_lanes(own, half):
    lane = jnp.where(holds_first(), 0 if own else half, half if own else 0)
    return pl.ds(pl.multiple_of(lane, half), half)


def row_parts(row_count):
    eighth = row_count // 8
    if eighth % 128:
        return [(0, row_count)]
    sizes = [eighth, 2 * eighth, 2 * eighth, 2 * eighth, eighth]
    return [(sum(sizes[:n]), size) for n, size in enumerate(sizes)]


def write_state(keep, send, acc, rank, blocks_of):
    half = acc.shape[1] // 2
    is_first = holds_first()
    at = 0
    for k in range(acc.shape[0] // rank):
        low = acc[k * rank : (k + 1) * rank, :half]
        high = acc[k * rank : (k + 1) * rank, half:]
        keep[at : at + rank, :] = jnp.where(is_first, low, high)
        send[at : at + rank, :] = jnp.where(is_first, high, low)
        at += rank
        for rows in pack(blocks_of(k)):
            keep[at : at + rows.shape[0], :] = rows
            send[at : at + rows.shape[0], :] = rows
            at += rows.shape[0]


def local_kernel(dims, parts, ahead, count_ref, x_hbm, w_hbm, u_hbm, q_hbm, node_ref, *refs):
    levels, rank, base_bits = dims
    keep, send, g_ref, nodes_out, x_all, w_all, u_all, q_all, c_acc, sems, w_sem, node_sems = refs
    position = lax.axis_index("leaf")

    def copies(n):
        part = pl.ds(*parts[n])
        pairs = [(u_hbm.at[:, part], u_all.at[:, part]), (x_hbm.at[part], x_all.at[part])]
        pairs.append((q_hbm.at[:, part], q_all.at[:, part]))
        return [pltpu.make_async_copy(a, b, sems.at[n, i]) for i, (a, b) in enumerate(pairs)]

    def node_copy(k):
        index = 2**levels - 2 ** (levels - k) + jnp.right_shift(position, base_bits + k + 1)
        return pltpu.make_async_copy(node_ref.at[index], nodes_out.at[k], node_sems.at[k])

    w_copy = pltpu.make_async_copy(w_hbm, w_all, w_sem)
    for n in range(ahead):
        for copy in copies(n):
            copy.start()
    for k in range(levels):
        node_copy(k).start()

    for n, (first, size) in enumerate(parts):
        @pl.when(position >= 0)
        def _():
            if n + ahead < len(parts):
                for copy in copies(n + ahead):
                    copy.start()
            if n + ahead == len(parts):
                w_copy.start()
            for copy in copies(n):
                copy.wait()
            part = pl.ds(first, size)
            place = first + lax.broadcasted_iota(jnp.int32, (1, size), 1)
            u = jnp.where(place < count_ref[:1, :1], u_all[:, part], 0.0)
            c = dot(u, x_all[part, :])
            g = dot(u, q_all[:, part], ((1,), (1,)))
            c_acc[...] = c if n == 0 else c_acc[...] + c
            g_ref[...] = g if n == 0 else g_ref[...] + g

    def blocks(k):
        lane = slice(k * rank, (k + 1) * rank)
        return [g_ref[i * rank : (i + 1) * rank, lane] for i in range(k + 1, levels)]

    write_state(keep, send, c_acc, rank, blocks)
    for k in range(levels):
        node_copy(k).wait()
    w_copy.wait()


def side_kernel(count_ref, w_ref, u_ref, k_ref):
    place = lax.broadcasted_iota(jnp.int32, (1, u_ref.shape[1]), 1)
    k_ref[...] = dot(jnp.where(place < count_ref[:1, :1], u_ref[...], 0.0), w_ref[...])


def side_state_kernel(dims, k_ref, g_ref, after_ref, keep, send):
    del after_ref
    levels, rank = dims

    def blocks(k):
        row = slice(k * rank, (k + 1) * rank)
        return [g_ref[row, j * rank : (j + 1) * rank] for j in range(k, levels)]

    write_state(keep, send, k_ref, rank, blocks)


def side_first_kernel(at, own_ref, sib_ref, after_ref, *out_refs):
    del after_ref
    for out_ref in out_refs:
        rows = out_ref.shape[0]
        out_ref[...] = own_ref[at : at + rows, :] + sib_ref[at : at + rows, :]
        at += rows


def side_join_kernel(first, fresh_ref, sent_ref, got_ref, after_ref, *refs):
    del after_ref
    *top_ref, out_ref = refs
    at, rows = fresh_ref.shape[0], got_ref.shape[0]
    out_ref[:at, :] = fresh_ref[...]
    out_ref[at : at + first, :] = got_ref[:first, :]
    if first < rows:
        out_ref[at + first : at + rows, :] = sent_ref[first:, :] + got_ref[first:, :]
    if top_ref:
        out_ref[at + rows :, :] = top_ref[0][...]


def side_top_kernel(sent_ref, got_ref, after_ref, out_ref):
    del after_ref
    at = sent_ref.shape[0] - out_ref.shape[0]
    out_ref[...] = sent_ref[at:, :] + got_ref[at:, :]


def level_kernel(dims, level, own_ref, sib_ref, nodes_ref, *refs):
    levels, rank, base_bits, placed = dims
    z_ref, *out_refs = refs[placed:]
    is_lower = jnp.right_shift(lax.axis_index("leaf"), base_bits + level) % 2 == 0
    own, sib = own_ref[:rank, :], sib_ref[:rank, :]
    both = jnp.concatenate([jnp.where(is_lower, own, sib), jnp.where(is_lower, sib, own)], 0)
    mixed = dot(nodes_ref[level], both)
    z_own = jnp.where(is_lower, mixed[:rank], mixed[rank:])
    z_sib = jnp.where(is_lower, mixed[rank:], mixed[:rank])
    z_ref[:rank, :] = z_own
    z_ref[rank:, :] = z_sib
    if not out_refs:
        return
    (out_ref,) = out_refs
    count = levels - 1 - level
    h_own = unpack(own_ref, rank, count, rank)
    h_sib = unpack(sib_ref, rank, count, rank)
    h_both = jnp.concatenate([jnp.concatenate(h_own, 0), jnp.concatenate(h_sib, 0)], 1)
    drop = dot(h_both, jnp.concatenate([z_own, z_sib], 0))

    def total(at, rows):
        return own_ref[at : at + rows, :] + sib_ref[at : at + rows, :]

    start = solve_rows(level, levels, rank)
    at = 0
    for i in range(count):
        out_ref[at : at + rank, :] = total(start + at, rank) - drop[i * rank : (i + 1) * rank]
        at += rank
        rest = solve_rows(level + 1 + i, levels, rank) - rank
        if rest:
            out_ref[at : at + rest, :] = total(start + at, rest)
            at += rest


def factor_terms(dims, k, c, side_ref, at, z_here, z_above):
    levels, rank, scale = dims
    blocks = unpack(side_ref, at + rank, levels - k, rank)
    z_here = jnp.concatenate([z_here, *z_above], 0)
    l_term = c - dot(jnp.concatenate(blocks, 1), z_here)
    return l_term * scale, side_ref[at : at + rank, :] * scale


def end_low_kernel(dims, pair, *refs):
    levels, rank, _ = dims
    solves, z_refs = refs[:levels], refs[levels : 2 * levels]
    sib_side, side_sent, side_got, own_solve, own_side = refs[2 * levels : 2 * levels + 5]
    *out_refs, side_sum = refs[2 * levels + 5 :]
    z_own = [z_ref[:rank, :] for z_ref in z_refs]

    low, rows = side_rows(1, levels, rank), side_sum.shape[0]
    side_sum[:low, :] = side_got[:low, :]
    side_sum[low:, :] = side_got[low:rows, :] + side_sent[low:rows, :]

    def write(out_ref, k, z_term, l_term, k_term):
        out_ref[k * rank : (k + 1) * rank, :] = z_term
        out_ref[(levels + k) * rank : (levels + k + 1) * rank, :] = l_term
        out_ref[(2 * levels - 1 + k) * rank : (2 * levels + k) * rank, :] = k_term

    at = 0
    for k in range(levels - 1):
        z_sib = z_refs[k][rank:, :]
        where = (sib_side, 0) if k == 0 else (side_sum, at)
        at += side_rows(k, levels, rank) if k > 0 else 0
        parts = (z_own[k], *factor_terms(dims, k, solves[k][:rank, :], *where, z_sib, z_own[k + 1 :]))
        write(out_refs[-1], k, *parts)
        if pair:
            if k == 0:
                parts = (z_sib, *factor_terms(dims, 0, own_solve[:rank, :], own_side, 0, z_own[0], z_own[1:]))
            write(out_refs[0], k, *parts)
    for out_ref in out_refs:
        out_ref[(levels - 1) * rank : levels * rank, :] = z_own[-1]
        out_ref[(3 * levels - 2) * rank : (3 * levels - 1) * rank, :] = solves[-1][:rank, :]
        out_ref[(3 * levels - 1) * rank :, :] = z_refs[-1][rank:, :]


def end_top_kernel(sent_ref, got_ref, k_ref, h_ref):
    rank = k_ref.shape[0]
    k_ref[...] = sent_ref[:rank, :] + got_ref[:rank, :]
    h_ref[...] = sent_ref[rank:, :] + got_ref[rank:, :]


def whole(own_ref, other_ref, start, rows):
    is_first = holds_first()
    own, other = own_ref[start : start + rows, :], other_ref[start : start + rows, :]
    return jnp.concatenate([jnp.where(is_first, own, other), jnp.where(is_first, other, own)], 1)


class Sender:
    def __init__(self, sems):
        self.sems, self.copies = sems, []

    def send(self, source, target):
        copy = pltpu.make_async_copy(source, target, self.sems.at[len(self.copies)])
        copy.start()
        self.copies.append(copy)

    def wait(self):
        for copy in self.copies:
            copy.wait()


def halves(value):
    high = value.astype(jnp.bfloat16)
    return high, (value - high.astype(F32)).astype(jnp.bfloat16)


def stacked(value):
    return jnp.concatenate(halves(value), 0)


def dot_stacked(both, b, dims):
    rows = both.shape[0] // 2
    b_high, b_low = halves(b)
    wide = lax.dot_general(both, b_high, (dims, ((), ())), preferred_element_type=F32)
    rest = lax.dot_general(both[:rows], b_low, (dims, ((), ())), preferred_element_type=F32)
    return wide[:rows] + (wide[rows:] + rest)


def solution_kernel(dims, count_ref, x_ref, q_ref, *refs):
    own, rank, chunk = dims
    *z_refs, sol = refs
    half = sol.shape[1]
    if own:
        z = jnp.concatenate([z_ref[:rank, :] for z_ref in z_refs], 0)
    else:
        z = z_refs[0][: q_ref.shape[0], :]
    z_high, z_low = halves(z)
    z_both = jnp.concatenate([z_high, z_low], 1)
    lanes = half_lanes(own, half)
    dims = (((0,), (0,)), ((), ()))
    for i in range(x_ref.shape[0] // chunk):
        part = slice(i * chunk, (i + 1) * chunk)
        live = i * chunk + lax.broadcasted_iota(jnp.int32, (chunk, 1), 0) < count_ref[:1, :1]
        q_high, q_low = halves(q_ref[:, part])
        both = lax.dot_general(q_high, z_both, dims, preferred_element_type=F32)
        rest = lax.dot_general(q_low, z_high, dims, preferred_element_type=F32)
        x = x_ref[part, lanes] - (both[:, :half] + (both[:, half:] + rest))
        sol[part, :] = jnp.where(live, x, 0.0)


def other_kernel(dims, scale, count_ref, x_ref, q_ref, low_own, low_other, h_ref, sol, l_ref):
    solution_kernel(dims, count_ref, x_ref, q_ref, low_other, sol)
    wide, rank = l_ref.shape[0], dims[1]
    low = wide - rank
    at = wide + 2 * low
    (block,) = unpack(h_ref, 0, 1, rank)
    l_top = whole(low_own, low_other, at, rank) - dot(block, whole(low_own, low_other, at + rank, rank))
    l_ref[:low, :] = whole(low_own, low_other, wide, low)
    l_ref[low:, :] = l_top * scale


def factor_kernel(dims, count_ref, low_own, low_other, k_own, k_other, l_ref, x_own, x_other, w_ref, *refs):
    wide, scale, chunk = dims
    sol_out, left_out, right_out, left, right, sems = refs
    sender = Sender(sems)
    half = x_own.shape[1]
    sender.send(x_own, sol_out.at[:, half_lanes(True, half)])
    sender.send(x_other, sol_out.at[:, half_lanes(False, half)])
    rank = k_own.shape[0]
    low = wide - rank
    at = wide + 2 * low
    k_low = jnp.concatenate([low_own[wide + low : at, :], low_other[wide + low : at, :]], 1)
    k = jnp.concatenate([k_low, jnp.concatenate([k_own[...], k_other[...]], 1) * scale], 0)
    l, k = stacked(l_ref[...]), stacked(k)
    for i in range(w_ref.shape[0] // chunk):
        part, place = slice(i * chunk, (i + 1) * chunk), pl.ds(i * chunk, chunk)
        live = i * chunk + lax.broadcasted_iota(jnp.int32, (1, chunk), 1) < count_ref[:1, :1]
        left_now = dot_stacked(l, w_ref[part, :], ((1,), (1,)))
        left[:, part] = jnp.where(live, left_now, 0.0).astype(left.dtype)
        sender.send(left.at[:, place], left_out.at[:, place])
        x = jnp.concatenate([x_own[part, :], x_other[part, :]], 1)
        right[:, part] = dot_stacked(k, x, ((1,), (1,))).astype(right.dtype)
        sender.send(right.at[:, place], right_out.at[:, place])
    sender.wait()


def swapped(value, bit):
    mask = 2**bit
    pairs = [(source, source ^ mask) for source in range(lax.axis_size("leaf"))]
    return lax.ppermute(value, "leaf", pairs)


def shape(*sizes, dtype=F32):
    return jax.ShapeDtypeStruct(sizes, dtype)


def body(right_side, cotangent, coeff_basis, saved_basis, node_inverse, leaf_rows):
    row_count, col_count = right_side.shape
    levels, rank = coeff_basis.shape[:2]
    wide, order, half = levels * rank, 2 * rank, col_count // 2
    low, top = wide - rank, levels - 1
    base_bits = lax.axis_size("leaf").bit_length() - 1 - levels
    pair = base_bits == 0
    chunk = min(512, row_count)
    steps = row_count // chunk
    parts = row_parts(row_count)
    u_all = coeff_basis.reshape(wide, row_count)
    q_all = saved_basis.reshape(wide, row_count)

    vmem = pl.BlockSpec(memory_space=pltpu.VMEM)
    anywhere = pl.BlockSpec(memory_space=pl.ANY)
    small = pltpu.CompilerParams(vmem_limit_bytes=4 * MIB)
    large = pltpu.CompilerParams(vmem_limit_bytes=20 * MIB)

    def call(kernel, name, out_shape, *operands, out_specs=vmem, scratch=(), params=small, cost=None, **options):
        if isinstance(out_shape, list) and out_specs is vmem:
            out_specs = [vmem] * len(out_shape)
        if cost is not None:
            options["cost_estimate"] = pl.CostEstimate(flops=cost, bytes_accessed=MIB, transcendentals=0)
        return pl.pallas_call(
            kernel,
            out_shape=out_shape,
            in_specs=[vmem] * len(operands),
            out_specs=out_specs,
            scratch_shapes=list(scratch),
            compiler_params=params,
            name=name,
            **options,
        )(*operands)

    n_solve = sum(solve_rows(k, levels, rank) for k in range(levels))
    n_side = [side_rows(k, levels, rank) for k in range(levels)]
    arrays = (right_side, cotangent, u_all, q_all)
    outs = [shape(n_solve, half), shape(n_solve, half), shape(wide, wide), shape(levels, order, order)]
    outs += [shape(*a.shape) for a in arrays]
    count = jnp.broadcast_to(leaf_rows[:, None], (8, 128))
    hbm = [pltpu.with_memory_space_constraint(a, pltpu.HBM) for a in (*arrays, node_inverse)]
    solve, solve_send, products, nodes, x_vmem, w_vmem, u_vmem, q_vmem = pl.pallas_call(
        functools.partial(local_kernel, (levels, rank, base_bits), parts, min(3, len(parts))),
        out_shape=outs,
        in_specs=[vmem] + [anywhere] * 5,
        out_specs=[vmem] * 8,
        scratch_shapes=[
            pltpu.VMEM((wide, col_count), F32),
            pltpu.SemaphoreType.DMA((len(parts), 3)),
            pltpu.SemaphoreType.DMA,
            pltpu.SemaphoreType.DMA((levels,)),
        ],
        compiler_params=large,
        name="local_sums",
    )(count, *hbm)
    k_sums = call(
        side_kernel,
        "side_sums",
        shape(wide, col_count),
        count,
        w_vmem,
        u_vmem,
        params=large,
        cost=6 * wide * row_count * col_count,
    )

    def lowest(solve, solve_send):
        if pair:
            return solve, swapped(solve_send, 0)
        solve = solve + swapped(solve_send, 0)
        for bit in range(1, base_bits):
            solve = solve + swapped(solve, bit)
        return solve, swapped(solve, base_bits)

    solve, sib_solve = lowest(solve, solve_send)
    own_solve = solve
    solves, zs, fresh = [], [], {}
    for k in range(levels):
        if k > 0:
            sib_solve = swapped(solve, base_bits + k)
        solves.append(sib_solve)
        placed = []
        if k == 1:
            top_got = swapped(fresh[top], base_bits + top)
            sent = fresh[top - 1]
            got = swapped(sent, base_bits + top - 1)
        elif 1 < k < top:
            bit = top - k
            sent = call(
                functools.partial(side_join_kernel, n_side[bit + 1]),
                f"side_join_{bit}",
                shape(sum(n_side[bit:]), half),
                fresh[bit],
                sent,
                got,
                zs[-1],
                *([top_got] if k == 2 else []),
                cost=2 * 10**10,
            )
            got = swapped(sent, base_bits + bit)
            placed = [sent]
        elif k == top:
            top_sum = call(side_top_kernel, "side_top", shape(n_side[top], half), sent, got, zs[-1])
            top_got = swapped(top_sum, base_bits + top - 1)
            placed = [top_sum]
        out_shape = [shape(order, half)]
        if k < top:
            out_shape.append(shape(sum(solve_rows(i, levels, rank) for i in range(k + 1, levels)), half))
        outs = call(
            functools.partial(level_kernel, (levels, rank, base_bits, len(placed)), k),
            f"level_{k}",
            out_shape,
            solve,
            sib_solve,
            nodes,
            *placed,
            cost=2 * 10**10,
        )
        zs.append(outs[0])
        if k < top:
            solve = outs[1]
        if k == 0:
            side, side_send = call(
                functools.partial(side_state_kernel, (levels, rank)),
                "side_state",
                [shape(sum(n_side), half)] * 2,
                k_sums,
                products,
                outs[0],
            )
            side, sib_side = lowest(side, side_send)
            first = call(
                functools.partial(side_first_kernel, n_side[0]),
                "side_first",
                [shape(size, half) for size in n_side[1:]],
                side,
                sib_side,
                outs[0],
            )
            fresh = dict(enumerate(first, 1))

    dims = (levels, rank, 1.0 / col_count**0.5)
    copies = 2 if pair else 1
    *low_other, low_own = call(
        functools.partial(end_low_kernel, dims, pair),
        "end_low",
        [shape(wide + 2 * low + order, half)] * copies,
        *solves,
        *zs,
        sib_side,
        sent,
        got,
        own_solve,
        side,
        scratch=[pltpu.VMEM((sum(n_side[1:top]), half), F32)],
    )
    low_other = swapped(low_other[0] if pair else low_own, 0)
    k_own, h_top = call(
        end_top_kernel,
        "end_top",
        [shape(rank, half), shape(n_side[top] - rank, half)],
        top_sum,
        top_got,
        cost=2 * 10**10,
    )
    k_other = swapped(k_own, 0)

    sol_own = call(
        functools.partial(solution_kernel, (True, rank, chunk)),
        "solution_own",
        shape(row_count, half),
        count,
        x_vmem,
        q_vmem,
        *zs,
        params=large,
        cost=10**9,
    )
    sol_other, l_all = call(
        functools.partial(other_kernel, (False, rank, chunk), dims[2]),
        "solution_other",
        [shape(row_count, half), shape(wide, col_count)],
        count,
        x_vmem,
        q_vmem,
        low_own,
        low_other,
        h_top,
        params=large,
        cost=10**9,
    )
    grad = shape(wide, row_count, dtype=jnp.bfloat16)
    sol, left, right = call(
        functools.partial(factor_kernel, (wide, dims[2], chunk)),
        "factor_rows",
        [shape(row_count, col_count), grad, grad],
        count,
        low_own,
        low_other,
        k_own,
        k_other,
        l_all,
        sol_own,
        sol_other,
        w_vmem,
        out_specs=[anywhere] * 3,
        scratch=[pltpu.VMEM(grad.shape, grad.dtype)] * 2 + [pltpu.SemaphoreType.DMA((2 * steps + 2,))],
        params=large,
    )
    return sol, left.reshape(coeff_basis.shape), right.reshape(coeff_basis.shape)


def solution(mesh):
    in_specs = (
        P(("groups", "leaf"), None),
        P(("groups", "leaf"), None),
        P(None, None, ("groups", "leaf")),
        P(None, None, ("groups", "leaf")),
        P("groups", None, None),
        P(("groups", "leaf")),
    )
    out_specs = (
        P(("groups", "leaf"), None),
        P(None, None, ("groups", "leaf")),
        P(None, None, ("groups", "leaf")),
    )
    return jax.shard_map(body, mesh=mesh, in_specs=in_specs, out_specs=out_specs, check_vma=False)
```

```python
import functools

import jax
import jax.numpy as jnp
from jax import lax
from jax.experimental import pallas as pl
from jax.experimental.pallas import tpu as pltpu
from jax.sharding import PartitionSpec as P


HIGH = lax.Precision.HIGH
F32 = jnp.float32
MIB = 2**20


def dot(a, b, dims=((1,), (0,))):
    return lax.dot_general(a, b, (dims, ((), ())), precision=HIGH, preferred_element_type=F32)


def halves(value):
    high = value.astype(jnp.bfloat16)
    return high, (value - high.astype(F32)).astype(jnp.bfloat16)


def dot_joined(a, b):
    a_high, a_low = halves(a)
    b_high, b_low = halves(b)
    left = jnp.concatenate([a_high, a_high, a_low], 1)
    right = jnp.concatenate([b_high, b_low, b_high], 0)
    return jnp.dot(left, right, preferred_element_type=F32)


def pack(blocks):
    rows = []
    for i in range(0, len(blocks) - 1, 2):
        rows.append(jnp.concatenate([blocks[i], blocks[i + 1]], 1))
    if len(blocks) % 2:
        half = blocks[-1].shape[0] // 2
        rows.append(jnp.concatenate([blocks[-1][:half], blocks[-1][half:]], 1))
    return rows


def pack_rows(count, rank):
    return count // 2 * rank + count % 2 * (rank // 2)


def unpack(ref, start, count, rank):
    blocks = []
    for i in range(count):
        if i == count - 1 and count % 2:
            half = ref[start : start + rank // 2, :]
            blocks.append(jnp.concatenate([half[:, :rank], half[:, rank:]], 0))
        else:
            lane = i % 2 * rank
            blocks.append(ref[start : start + rank, lane : lane + rank])
            start += i % 2 * rank
    return blocks


def side_rows(level, levels, rank):
    return rank + pack_rows(levels - level, rank)


def solve_rows(level, levels, rank):
    return rank + pack_rows(levels - 1 - level, rank)


def holds_first():
    return lax.axis_index("leaf") % 2 == 0


def half_lanes(own, half):
    lane = jnp.where(holds_first(), 0 if own else half, half if own else 0)
    return pl.ds(pl.multiple_of(lane, half), half)


def row_parts(row_count):
    eighth = row_count // 8
    if eighth % 128:
        return [(0, row_count)]
    sizes = [eighth, 2 * eighth, 2 * eighth, 2 * eighth, eighth]
    return [(sum(sizes[:n]), size) for n, size in enumerate(sizes)]


def write_state(keep, send, acc, rank, blocks_of):
    half = acc.shape[1] // 2
    is_first = holds_first()
    at = 0
    for k in range(acc.shape[0] // rank):
        low = acc[k * rank : (k + 1) * rank, :half]
        high = acc[k * rank : (k + 1) * rank, half:]
        keep[at : at + rank, :] = jnp.where(is_first, low, high)
        send[at : at + rank, :] = jnp.where(is_first, high, low)
        at += rank
        for rows in pack(blocks_of(k)):
            keep[at : at + rows.shape[0], :] = rows
            send[at : at + rows.shape[0], :] = rows
            at += rows.shape[0]


def local_kernel(dims, parts, ahead, count_ref, x_hbm, w_hbm, u_hbm, q_hbm, node_ref, *refs):
    levels, rank, base_bits = dims
    keep, send, g_ref, nodes_out, x_all, w_all, u_all, q_all, c_acc, sems, w_sem, node_sems = refs
    position = lax.axis_index("leaf")

    def copies(n):
        part = pl.ds(*parts[n])
        pairs = [(u_hbm.at[:, part], u_all.at[:, part]), (x_hbm.at[part], x_all.at[part])]
        pairs.append((q_hbm.at[:, part], q_all.at[:, part]))
        return [pltpu.make_async_copy(a, b, sems.at[n, i]) for i, (a, b) in enumerate(pairs)]

    def node_copy(k):
        index = 2**levels - 2 ** (levels - k) + jnp.right_shift(position, base_bits + k + 1)
        return pltpu.make_async_copy(node_ref.at[index], nodes_out.at[k], node_sems.at[k])

    w_copy = pltpu.make_async_copy(w_hbm, w_all, w_sem)
    for n in range(ahead):
        for copy in copies(n):
            copy.start()
    for k in range(levels):
        node_copy(k).start()

    for n, (first, size) in enumerate(parts):
        @pl.when(position >= 0)
        def _():
            if n + ahead < len(parts):
                for copy in copies(n + ahead):
                    copy.start()
            if n + ahead == len(parts):
                w_copy.start()
            for copy in copies(n):
                copy.wait()
            part = pl.ds(first, size)
            place = first + lax.broadcasted_iota(jnp.int32, (1, size), 1)
            u = jnp.where(place < count_ref[:1, :1], u_all[:, part], 0.0)
            c = dot(u, x_all[part, :])
            g = dot(u, q_all[:, part], ((1,), (1,)))
            c_acc[...] = c if n == 0 else c_acc[...] + c
            g_ref[...] = g if n == 0 else g_ref[...] + g

    def blocks(k):
        lane = slice(k * rank, (k + 1) * rank)
        return [g_ref[i * rank : (i + 1) * rank, lane] for i in range(k + 1, levels)]

    write_state(keep, send, c_acc, rank, blocks)
    for k in range(levels):
        node_copy(k).wait()
    w_copy.wait()


def side_kernel(count_ref, w_ref, u_ref, k_ref):
    place = lax.broadcasted_iota(jnp.int32, (1, u_ref.shape[1]), 1)
    k_ref[...] = dot(jnp.where(place < count_ref[:1, :1], u_ref[...], 0.0), w_ref[...])


def side_state_kernel(dims, k_ref, g_ref, after_ref, keep, send):
    del after_ref
    levels, rank = dims

    def blocks(k):
        row = slice(k * rank, (k + 1) * rank)
        return [g_ref[row, j * rank : (j + 1) * rank] for j in range(k, levels)]

    write_state(keep, send, k_ref, rank, blocks)


def side_first_kernel(at, own_ref, sib_ref, after_ref, *out_refs):
    del after_ref
    for out_ref in out_refs:
        rows = out_ref.shape[0]
        out_ref[...] = own_ref[at : at + rows, :] + sib_ref[at : at + rows, :]
        at += rows


def side_join_kernel(first, fresh_ref, sent_ref, got_ref, after_ref, *refs):
    del after_ref
    *top_ref, out_ref = refs
    at, rows = fresh_ref.shape[0], got_ref.shape[0]
    out_ref[:at, :] = fresh_ref[...]
    out_ref[at : at + first, :] = got_ref[:first, :]
    if first < rows:
        out_ref[at + first : at + rows, :] = sent_ref[first:, :] + got_ref[first:, :]
    if top_ref:
        out_ref[at + rows :, :] = top_ref[0][...]


def side_top_kernel(sent_ref, got_ref, after_ref, out_ref):
    del after_ref
    at = sent_ref.shape[0] - out_ref.shape[0]
    out_ref[...] = sent_ref[at:, :] + got_ref[at:, :]


def level_kernel(dims, level, own_ref, sib_ref, nodes_ref, *refs):
    levels, rank, base_bits, placed = dims
    z_ref, *out_refs = refs[placed:]
    is_lower = jnp.right_shift(lax.axis_index("leaf"), base_bits + level) % 2 == 0
    own, sib = own_ref[:rank, :], sib_ref[:rank, :]
    both = jnp.concatenate([jnp.where(is_lower, own, sib), jnp.where(is_lower, sib, own)], 0)
    mixed = dot_joined(nodes_ref[level], both)
    z_own = jnp.where(is_lower, mixed[:rank], mixed[rank:])
    z_sib = jnp.where(is_lower, mixed[rank:], mixed[:rank])
    z_ref[:rank, :] = z_own
    z_ref[rank:, :] = z_sib
    if not out_refs:
        return
    (out_ref,) = out_refs
    count = levels - 1 - level
    h_own = unpack(own_ref, rank, count, rank)
    h_sib = unpack(sib_ref, rank, count, rank)
    h_both = jnp.concatenate([jnp.concatenate(h_own, 0), jnp.concatenate(h_sib, 0)], 1)
    drop = dot_joined(h_both, jnp.concatenate([z_own, z_sib], 0))

    def total(at, rows):
        return own_ref[at : at + rows, :] + sib_ref[at : at + rows, :]

    start = solve_rows(level, levels, rank)
    at = 0
    for i in range(count):
        out_ref[at : at + rank, :] = total(start + at, rank) - drop[i * rank : (i + 1) * rank]
        at += rank
        rest = solve_rows(level + 1 + i, levels, rank) - rank
        if rest:
            out_ref[at : at + rest, :] = total(start + at, rest)
            at += rest


def factor_terms(dims, k, c, side_ref, at, z_here, z_above):
    levels, rank, scale = dims
    blocks = unpack(side_ref, at + rank, levels - k, rank)
    z_here = jnp.concatenate([z_here, *z_above], 0)
    l_term = c - dot(jnp.concatenate(blocks, 1), z_here)
    return l_term * scale, side_ref[at : at + rank, :] * scale


def end_low_kernel(dims, pair, *refs):
    levels, rank, _ = dims
    solves, z_refs = refs[:levels], refs[levels : 2 * levels]
    sib_side, side_sent, side_got, own_solve, own_side = refs[2 * levels : 2 * levels + 5]
    *out_refs, side_sum = refs[2 * levels + 5 :]
    z_own = [z_ref[:rank, :] for z_ref in z_refs]

    low, rows = side_rows(1, levels, rank), side_sum.shape[0]
    side_sum[:low, :] = side_got[:low, :]
    side_sum[low:, :] = side_got[low:rows, :] + side_sent[low:rows, :]

    def write(out_ref, k, z_term, l_term, k_term):
        out_ref[k * rank : (k + 1) * rank, :] = z_term
        out_ref[(levels + k) * rank : (levels + k + 1) * rank, :] = l_term
        out_ref[(2 * levels - 1 + k) * rank : (2 * levels + k) * rank, :] = k_term

    at = 0
    for k in range(levels - 1):
        z_sib = z_refs[k][rank:, :]
        where = (sib_side, 0) if k == 0 else (side_sum, at)
        at += side_rows(k, levels, rank) if k > 0 else 0
        parts = (z_own[k], *factor_terms(dims, k, solves[k][:rank, :], *where, z_sib, z_own[k + 1 :]))
        write(out_refs[-1], k, *parts)
        if pair:
            if k == 0:
                parts = (z_sib, *factor_terms(dims, 0, own_solve[:rank, :], own_side, 0, z_own[0], z_own[1:]))
            write(out_refs[0], k, *parts)
    for out_ref in out_refs:
        out_ref[(levels - 1) * rank : levels * rank, :] = z_own[-1]
        out_ref[(3 * levels - 2) * rank : (3 * levels - 1) * rank, :] = solves[-1][:rank, :]
        out_ref[(3 * levels - 1) * rank :, :] = z_refs[-1][rank:, :]


def end_top_kernel(sent_ref, got_ref, k_ref, h_ref):
    rank = k_ref.shape[0]
    k_ref[...] = sent_ref[:rank, :] + got_ref[:rank, :]
    h_ref[...] = sent_ref[rank:, :] + got_ref[rank:, :]


def whole(own_ref, other_ref, start, rows):
    is_first = holds_first()
    own, other = own_ref[start : start + rows, :], other_ref[start : start + rows, :]
    return jnp.concatenate([jnp.where(is_first, own, other), jnp.where(is_first, other, own)], 1)


class Sender:
    def __init__(self, sems):
        self.sems, self.copies = sems, []

    def send(self, source, target):
        copy = pltpu.make_async_copy(source, target, self.sems.at[len(self.copies)])
        copy.start()
        self.copies.append(copy)

    def wait(self):
        for copy in self.copies:
            copy.wait()


def solution_kernel(dims, count_ref, x_ref, q_ref, *refs):
    own, rank, chunk = dims
    *z_refs, sol = refs
    half = sol.shape[1]
    if own:
        z = jnp.concatenate([z_ref[:rank, :] for z_ref in z_refs], 0)
    else:
        z = z_refs[0][: q_ref.shape[0], :]
    z_high, z_low = halves(z)
    z_both = jnp.concatenate([z_high, z_low], 1)
    lanes = half_lanes(own, half)
    dims = (((0,), (0,)), ((), ()))
    for i in range(x_ref.shape[0] // chunk):
        part = slice(i * chunk, (i + 1) * chunk)
        live = i * chunk + lax.broadcasted_iota(jnp.int32, (chunk, 1), 0) < count_ref[:1, :1]
        q_high, q_low = halves(q_ref[:, part])
        both = lax.dot_general(q_high, z_both, dims, preferred_element_type=F32)
        rest = lax.dot_general(q_low, z_high, dims, preferred_element_type=F32)
        x = x_ref[part, lanes] - (both[:, :half] + (both[:, half:] + rest))
        sol[part, :] = jnp.where(live, x, 0.0)


def factor_kernel(dims, count_ref, low_own, low_other, k_own, k_other, h_ref, x_own, x_other, w_ref, *refs):
    wide, scale, chunk = dims
    sol_out, left_out, right_out, left, right, sems = refs
    sender = Sender(sems)
    half = x_own.shape[1]
    sender.send(x_own, sol_out.at[:, half_lanes(True, half)])
    sender.send(x_other, sol_out.at[:, half_lanes(False, half)])
    rank = k_own.shape[0]
    low = wide - rank
    at = wide + 2 * low
    (block,) = unpack(h_ref, 0, 1, rank)
    l_top = whole(low_own, low_other, at, rank) - dot(block, whole(low_own, low_other, at + rank, rank))
    l = jnp.concatenate([whole(low_own, low_other, wide, low), l_top * scale], 0)
    k_low = jnp.concatenate([low_own[wide + low : at, :], low_other[wide + low : at, :]], 1)
    k = jnp.concatenate([k_low, jnp.concatenate([k_own[...], k_other[...]], 1) * scale], 0)
    for i in range(w_ref.shape[0] // chunk):
        part, place = slice(i * chunk, (i + 1) * chunk), pl.ds(i * chunk, chunk)
        live = i * chunk + lax.broadcasted_iota(jnp.int32, (1, chunk), 1) < count_ref[:1, :1]
        left_now = dot(l, w_ref[part, :], ((1,), (1,)))
        left[:, part] = jnp.where(live, left_now, 0.0).astype(left.dtype)
        sender.send(left.at[:, place], left_out.at[:, place])
        x = jnp.concatenate([x_own[part, :], x_other[part, :]], 1)
        right[:, part] = dot(k, x, ((1,), (1,))).astype(right.dtype)
        sender.send(right.at[:, place], right_out.at[:, place])
    sender.wait()


def swapped(value, bit):
    mask = 2**bit
    pairs = [(source, source ^ mask) for source in range(lax.axis_size("leaf"))]
    return lax.ppermute(value, "leaf", pairs)


def shape(*sizes, dtype=F32):
    return jax.ShapeDtypeStruct(sizes, dtype)


def body(right_side, cotangent, coeff_basis, saved_basis, node_inverse, leaf_rows):
    row_count, col_count = right_side.shape
    levels, rank = coeff_basis.shape[:2]
    wide, order, half = levels * rank, 2 * rank, col_count // 2
    low, top = wide - rank, levels - 1
    base_bits = lax.axis_size("leaf").bit_length() - 1 - levels
    pair = base_bits == 0
    chunk = min(512, row_count)
    steps = row_count // chunk
    parts = row_parts(row_count)
    u_all = coeff_basis.reshape(wide, row_count)
    q_all = saved_basis.reshape(wide, row_count)

    vmem = pl.BlockSpec(memory_space=pltpu.VMEM)
    anywhere = pl.BlockSpec(memory_space=pl.ANY)
    small = pltpu.CompilerParams(vmem_limit_bytes=4 * MIB)
    large = pltpu.CompilerParams(vmem_limit_bytes=20 * MIB)

    def call(kernel, name, out_shape, *operands, out_specs=vmem, scratch=(), params=small, cost=None, **options):
        if isinstance(out_shape, list) and out_specs is vmem:
            out_specs = [vmem] * len(out_shape)
        if cost is not None:
            options["cost_estimate"] = pl.CostEstimate(flops=cost, bytes_accessed=MIB, transcendentals=0)
        return pl.pallas_call(
            kernel,
            out_shape=out_shape,
            in_specs=[vmem] * len(operands),
            out_specs=out_specs,
            scratch_shapes=list(scratch),
            compiler_params=params,
            name=name,
            **options,
        )(*operands)

    n_solve = sum(solve_rows(k, levels, rank) for k in range(levels))
    n_side = [side_rows(k, levels, rank) for k in range(levels)]
    arrays = (right_side, cotangent, u_all, q_all)
    outs = [shape(n_solve, half), shape(n_solve, half), shape(wide, wide), shape(levels, order, order)]
    outs += [shape(*a.shape) for a in arrays]
    count = jnp.broadcast_to(leaf_rows[:, None], (8, 128))
    hbm = [pltpu.with_memory_space_constraint(a, pltpu.HBM) for a in (*arrays, node_inverse)]
    solve, solve_send, products, nodes, x_vmem, w_vmem, u_vmem, q_vmem = pl.pallas_call(
        functools.partial(local_kernel, (levels, rank, base_bits), parts, min(3, len(parts))),
        out_shape=outs,
        in_specs=[vmem] + [anywhere] * 5,
        out_specs=[vmem] * 8,
        scratch_shapes=[
            pltpu.VMEM((wide, col_count), F32),
            pltpu.SemaphoreType.DMA((len(parts), 3)),
            pltpu.SemaphoreType.DMA,
            pltpu.SemaphoreType.DMA((levels,)),
        ],
        compiler_params=large,
        name="local_sums",
    )(count, *hbm)
    k_sums = call(
        side_kernel,
        "side_sums",
        shape(wide, col_count),
        count,
        w_vmem,
        u_vmem,
        params=large,
        cost=6 * wide * row_count * col_count,
    )

    def lowest(solve, solve_send):
        if pair:
            return solve, swapped(solve_send, 0)
        solve = solve + swapped(solve_send, 0)
        for bit in range(1, base_bits):
            solve = solve + swapped(solve, bit)
        return solve, swapped(solve, base_bits)

    solve, sib_solve = lowest(solve, solve_send)
    own_solve = solve
    solves, zs, fresh = [], [], {}
    for k in range(levels):
        if k > 0:
            sib_solve = swapped(solve, base_bits + k)
        solves.append(sib_solve)
        placed = []
        if k == 1:
            top_got = swapped(fresh[top], base_bits + top)
            sent = fresh[top - 1]
            got = swapped(sent, base_bits + top - 1)
        elif 1 < k < top:
            bit = top - k
            sent = call(
                functools.partial(side_join_kernel, n_side[bit + 1]),
                f"side_join_{bit}",
                shape(sum(n_side[bit:]), half),
                fresh[bit],
                sent,
                got,
                zs[-1],
                *([top_got] if k == 2 else []),
                cost=2 * 10**10,
            )
            got = swapped(sent, base_bits + bit)
            placed = [sent]
        elif k == top:
            top_sum = call(side_top_kernel, "side_top", shape(n_side[top], half), sent, got, zs[-1])
            top_got = swapped(top_sum, base_bits + top - 1)
            placed = [top_sum]
        out_shape = [shape(order, half)]
        if k < top:
            out_shape.append(shape(sum(solve_rows(i, levels, rank) for i in range(k + 1, levels)), half))
        outs = call(
            functools.partial(level_kernel, (levels, rank, base_bits, len(placed)), k),
            f"level_{k}",
            out_shape,
            solve,
            sib_solve,
            nodes,
            *placed,
            cost=2 * 10**10,
        )
        zs.append(outs[0])
        if k < top:
            solve = outs[1]
        if k == 0:
            side, side_send = call(
                functools.partial(side_state_kernel, (levels, rank)),
                "side_state",
                [shape(sum(n_side), half)] * 2,
                k_sums,
                products,
                outs[0],
            )
            side, sib_side = lowest(side, side_send)
            first = call(
                functools.partial(side_first_kernel, n_side[0]),
                "side_first",
                [shape(size, half) for size in n_side[1:]],
                side,
                sib_side,
                outs[0],
            )
            fresh = dict(enumerate(first, 1))

    dims = (levels, rank, 1.0 / col_count**0.5)
    copies = 2 if pair else 1
    *low_other, low_own = call(
        functools.partial(end_low_kernel, dims, pair),
        "end_low",
        [shape(wide + 2 * low + order, half)] * copies,
        *solves,
        *zs,
        sib_side,
        sent,
        got,
        own_solve,
        side,
        scratch=[pltpu.VMEM((sum(n_side[1:top]), half), F32)],
    )
    low_other = swapped(low_other[0] if pair else low_own, 0)
    k_own, h_top = call(
        end_top_kernel,
        "end_top",
        [shape(rank, half), shape(n_side[top] - rank, half)],
        top_sum,
        top_got,
        cost=2 * 10**10,
    )
    k_other = swapped(k_own, 0)

    sol_own = call(
        functools.partial(solution_kernel, (True, rank, chunk)),
        "solution_own",
        shape(row_count, half),
        count,
        x_vmem,
        q_vmem,
        *zs,
        params=large,
        cost=10**9,
    )
    sol_other = call(
        functools.partial(solution_kernel, (False, rank, chunk)),
        "solution_other",
        shape(row_count, half),
        count,
        x_vmem,
        q_vmem,
        low_other,
        params=large,
        cost=10**9,
    )
    grad = shape(wide, row_count, dtype=jnp.bfloat16)
    sol, left, right = call(
        functools.partial(factor_kernel, (wide, dims[2], chunk)),
        "factor_rows",
        [shape(row_count, col_count), grad, grad],
        count,
        low_own,
        low_other,
        k_own,
        k_other,
        h_top,
        sol_own,
        sol_other,
        w_vmem,
        out_specs=[anywhere] * 3,
        scratch=[pltpu.VMEM(grad.shape, grad.dtype)] * 2 + [pltpu.SemaphoreType.DMA((2 * steps + 2,))],
        params=large,
    )
    return sol, left.reshape(coeff_basis.shape), right.reshape(coeff_basis.shape)


def solution(mesh):
    in_specs = (
        P(("groups", "leaf"), None),
        P(("groups", "leaf"), None),
        P(None, None, ("groups", "leaf")),
        P(None, None, ("groups", "leaf")),
        P("groups", None, None),
        P(("groups", "leaf")),
    )
    out_specs = (
        P(("groups", "leaf"), None),
        P(None, None, ("groups", "leaf")),
        P(None, None, ("groups", "leaf")),
    )
    return jax.shard_map(body, mesh=mesh, in_specs=in_specs, out_specs=out_specs, check_vma=False)
```

```python
import functools

import jax
import jax.numpy as jnp
from jax import lax
from jax.experimental import pallas as pl
from jax.experimental.pallas import tpu as pltpu
from jax.sharding import PartitionSpec as P


HIGH = lax.Precision.HIGH
F32 = jnp.float32
MIB = 2**20


def dot(a, b, dims=((1,), (0,))):
    return lax.dot_general(a, b, (dims, ((), ())), precision=HIGH, preferred_element_type=F32)


def halves(value):
    high = value.astype(jnp.bfloat16)
    return high, (value - high.astype(F32)).astype(jnp.bfloat16)


def dot_joined(a, b):
    a_high, a_low = halves(a)
    b_high, b_low = halves(b)
    left = jnp.concatenate([a_high, a_high, a_low], 1)
    right = jnp.concatenate([b_high, b_low, b_high], 0)
    return jnp.dot(left, right, preferred_element_type=F32)


def pack(blocks):
    rows = []
    for i in range(0, len(blocks) - 1, 2):
        rows.append(jnp.concatenate([blocks[i], blocks[i + 1]], 1))
    if len(blocks) % 2:
        half = blocks[-1].shape[0] // 2
        rows.append(jnp.concatenate([blocks[-1][:half], blocks[-1][half:]], 1))
    return rows


def pack_rows(count, rank):
    return count // 2 * rank + count % 2 * (rank // 2)


def unpack(ref, start, count, rank):
    blocks = []
    for i in range(count):
        if i == count - 1 and count % 2:
            half = ref[start : start + rank // 2, :]
            blocks.append(jnp.concatenate([half[:, :rank], half[:, rank:]], 0))
        else:
            lane = i % 2 * rank
            blocks.append(ref[start : start + rank, lane : lane + rank])
            start += i % 2 * rank
    return blocks


def side_rows(level, levels, rank):
    return rank + pack_rows(levels - level, rank)


def solve_rows(level, levels, rank):
    return rank + pack_rows(levels - 1 - level, rank)


def holds_first():
    return lax.axis_index("leaf") % 2 == 0


def half_lanes(own, half):
    lane = jnp.where(holds_first(), 0 if own else half, half if own else 0)
    return pl.ds(pl.multiple_of(lane, half), half)


def row_parts(row_count):
    eighth = row_count // 8
    if eighth % 128:
        return [(0, row_count)]
    sizes = [eighth, 2 * eighth, 2 * eighth, 2 * eighth, eighth]
    return [(sum(sizes[:n]), size) for n, size in enumerate(sizes)]


def last_row_parts(row_count):
    eighth = row_count // 8
    if eighth % 128:
        return [(0, row_count)]
    sizes = [2 * eighth, 2 * eighth, 3 * eighth, eighth]
    return [(sum(sizes[:n]), size) for n, size in enumerate(sizes)]


def write_state(keep, send, acc, rank, blocks_of):
    half = acc.shape[1] // 2
    is_first = holds_first()
    at = 0
    for k in range(acc.shape[0] // rank):
        low = acc[k * rank : (k + 1) * rank, :half]
        high = acc[k * rank : (k + 1) * rank, half:]
        keep[at : at + rank, :] = jnp.where(is_first, low, high)
        send[at : at + rank, :] = jnp.where(is_first, high, low)
        at += rank
        for rows in pack(blocks_of(k)):
            keep[at : at + rows.shape[0], :] = rows
            send[at : at + rows.shape[0], :] = rows
            at += rows.shape[0]


def local_kernel(dims, parts, ahead, count_ref, x_hbm, w_hbm, u_hbm, q_hbm, node_ref, *refs):
    levels, rank, base_bits = dims
    keep, send, g_ref, nodes_out, x_all, w_all, u_all, q_all, c_acc, sems, w_sem, node_sems = refs
    position = lax.axis_index("leaf")

    def copies(n):
        part = pl.ds(*parts[n])
        pairs = [(u_hbm.at[:, part], u_all.at[:, part]), (x_hbm.at[part], x_all.at[part])]
        pairs.append((q_hbm.at[:, part], q_all.at[:, part]))
        return [pltpu.make_async_copy(a, b, sems.at[n, i]) for i, (a, b) in enumerate(pairs)]

    def node_copy(k):
        index = 2**levels - 2 ** (levels - k) + jnp.right_shift(position, base_bits + k + 1)
        return pltpu.make_async_copy(node_ref.at[index], nodes_out.at[k], node_sems.at[k])

    w_copy = pltpu.make_async_copy(w_hbm, w_all, w_sem)
    for n in range(ahead):
        for copy in copies(n):
            copy.start()
    for k in range(levels):
        node_copy(k).start()

    for n, (first, size) in enumerate(parts):
        @pl.when(position >= 0)
        def _():
            if n + ahead < len(parts):
                for copy in copies(n + ahead):
                    copy.start()
            if n + ahead == len(parts):
                w_copy.start()
            for copy in copies(n):
                copy.wait()
            part = pl.ds(first, size)
            place = first + lax.broadcasted_iota(jnp.int32, (1, size), 1)
            u = jnp.where(place < count_ref[:1, :1], u_all[:, part], 0.0)
            c = dot(u, x_all[part, :])
            g = dot(u, q_all[:, part], ((1,), (1,)))
            c_acc[...] = c if n == 0 else c_acc[...] + c
            g_ref[...] = g if n == 0 else g_ref[...] + g

    def blocks(k):
        lane = slice(k * rank, (k + 1) * rank)
        return [g_ref[i * rank : (i + 1) * rank, lane] for i in range(k + 1, levels)]

    write_state(keep, send, c_acc, rank, blocks)
    for k in range(levels):
        node_copy(k).wait()
    w_copy.wait()


def side_kernel(count_ref, w_ref, u_ref, k_ref):
    place = lax.broadcasted_iota(jnp.int32, (1, u_ref.shape[1]), 1)
    k_ref[...] = dot(jnp.where(place < count_ref[:1, :1], u_ref[...], 0.0), w_ref[...])


def side_state_kernel(dims, k_ref, g_ref, after_ref, keep, send):
    del after_ref
    levels, rank = dims

    def blocks(k):
        row = slice(k * rank, (k + 1) * rank)
        return [g_ref[row, j * rank : (j + 1) * rank] for j in range(k, levels)]

    write_state(keep, send, k_ref, rank, blocks)


def side_first_kernel(at, own_ref, sib_ref, after_ref, *out_refs):
    del after_ref
    for out_ref in out_refs:
        rows = out_ref.shape[0]
        out_ref[...] = own_ref[at : at + rows, :] + sib_ref[at : at + rows, :]
        at += rows


def side_join_kernel(first, fresh_ref, sent_ref, got_ref, after_ref, *refs):
    del after_ref
    *top_ref, out_ref = refs
    at, rows = fresh_ref.shape[0], got_ref.shape[0]
    out_ref[:at, :] = fresh_ref[...]
    out_ref[at : at + first, :] = got_ref[:first, :]
    if first < rows:
        out_ref[at + first : at + rows, :] = sent_ref[first:, :] + got_ref[first:, :]
    if top_ref:
        out_ref[at + rows :, :] = top_ref[0][...]


def side_top_kernel(sent_ref, got_ref, after_ref, out_ref):
    del after_ref
    at = sent_ref.shape[0] - out_ref.shape[0]
    out_ref[...] = sent_ref[at:, :] + got_ref[at:, :]


def level_kernel(dims, level, own_ref, sib_ref, nodes_ref, *refs):
    levels, rank, base_bits, placed = dims
    z_ref, *out_refs = refs[placed:]
    is_lower = jnp.right_shift(lax.axis_index("leaf"), base_bits + level) % 2 == 0
    own, sib = own_ref[:rank, :], sib_ref[:rank, :]
    both = jnp.concatenate([jnp.where(is_lower, own, sib), jnp.where(is_lower, sib, own)], 0)
    mixed = dot_joined(nodes_ref[level], both)
    z_own = jnp.where(is_lower, mixed[:rank], mixed[rank:])
    z_sib = jnp.where(is_lower, mixed[rank:], mixed[:rank])
    z_ref[:rank, :] = z_own
    z_ref[rank:, :] = z_sib
    if not out_refs:
        return
    (out_ref,) = out_refs
    count = levels - 1 - level
    h_own = unpack(own_ref, rank, count, rank)
    h_sib = unpack(sib_ref, rank, count, rank)
    h_both = jnp.concatenate([jnp.concatenate(h_own, 0), jnp.concatenate(h_sib, 0)], 1)
    drop = dot_joined(h_both, jnp.concatenate([z_own, z_sib], 0))

    def total(at, rows):
        return own_ref[at : at + rows, :] + sib_ref[at : at + rows, :]

    start = solve_rows(level, levels, rank)
    at = 0
    for i in range(count):
        out_ref[at : at + rank, :] = total(start + at, rank) - drop[i * rank : (i + 1) * rank]
        at += rank
        rest = solve_rows(level + 1 + i, levels, rank) - rank
        if rest:
            out_ref[at : at + rest, :] = total(start + at, rest)
            at += rest


def factor_terms(dims, k, c, side_ref, at, z_here, z_above):
    levels, rank, scale = dims
    blocks = unpack(side_ref, at + rank, levels - k, rank)
    z_here = jnp.concatenate([z_here, *z_above], 0)
    l_term = c - dot(jnp.concatenate(blocks, 1), z_here)
    return l_term * scale, side_ref[at : at + rank, :] * scale


def end_low_kernel(dims, pair, *refs):
    levels, rank, _ = dims
    solves, z_refs = refs[:levels], refs[levels : 2 * levels]
    sib_side, side_sent, side_got, own_solve, own_side = refs[2 * levels : 2 * levels + 5]
    *out_refs, side_sum = refs[2 * levels + 5 :]
    z_own = [z_ref[:rank, :] for z_ref in z_refs]

    low, rows = side_rows(1, levels, rank), side_sum.shape[0]
    side_sum[:low, :] = side_got[:low, :]
    side_sum[low:, :] = side_got[low:rows, :] + side_sent[low:rows, :]

    def write(out_ref, k, z_term, l_term, k_term):
        out_ref[k * rank : (k + 1) * rank, :] = z_term
        out_ref[(levels + k) * rank : (levels + k + 1) * rank, :] = l_term
        out_ref[(2 * levels - 1 + k) * rank : (2 * levels + k) * rank, :] = k_term

    at = 0
    for k in range(levels - 1):
        z_sib = z_refs[k][rank:, :]
        where = (sib_side, 0) if k == 0 else (side_sum, at)
        at += side_rows(k, levels, rank) if k > 0 else 0
        parts = (z_own[k], *factor_terms(dims, k, solves[k][:rank, :], *where, z_sib, z_own[k + 1 :]))
        write(out_refs[-1], k, *parts)
        if pair:
            if k == 0:
                parts = (z_sib, *factor_terms(dims, 0, own_solve[:rank, :], own_side, 0, z_own[0], z_own[1:]))
            write(out_refs[0], k, *parts)
    for out_ref in out_refs:
        out_ref[(levels - 1) * rank : levels * rank, :] = z_own[-1]
        out_ref[(3 * levels - 2) * rank : (3 * levels - 1) * rank, :] = solves[-1][:rank, :]
        out_ref[(3 * levels - 1) * rank :, :] = z_refs[-1][rank:, :]


def end_top_kernel(sent_ref, got_ref, k_ref, h_ref):
    rank = k_ref.shape[0]
    k_ref[...] = sent_ref[:rank, :] + got_ref[:rank, :]
    h_ref[...] = sent_ref[rank:, :] + got_ref[rank:, :]


def whole(own_ref, other_ref, start, rows):
    is_first = holds_first()
    own, other = own_ref[start : start + rows, :], other_ref[start : start + rows, :]
    return jnp.concatenate([jnp.where(is_first, own, other), jnp.where(is_first, other, own)], 1)


class Sender:
    def __init__(self, sems):
        self.sems, self.copies = sems, []

    def send(self, source, target):
        copy = pltpu.make_async_copy(source, target, self.sems.at[len(self.copies)])
        copy.start()
        self.copies.append(copy)

    def wait(self):
        for copy in self.copies:
            copy.wait()


def solution_kernel(dims, count_ref, x_ref, q_ref, *refs):
    own, rank, chunk = dims
    *z_refs, sol = refs
    half = sol.shape[1]
    if own:
        z = jnp.concatenate([z_ref[:rank, :] for z_ref in z_refs], 0)
    else:
        z = z_refs[0][: q_ref.shape[0], :]
    z_high, z_low = halves(z)
    z_both = jnp.concatenate([z_high, z_low], 1)
    lanes = half_lanes(own, half)
    dims = (((0,), (0,)), ((), ()))
    for i in range(x_ref.shape[0] // chunk):
        part = slice(i * chunk, (i + 1) * chunk)
        live = i * chunk + lax.broadcasted_iota(jnp.int32, (chunk, 1), 0) < count_ref[:1, :1]
        q_high, q_low = halves(q_ref[:, part])
        both = lax.dot_general(q_high, z_both, dims, preferred_element_type=F32)
        rest = lax.dot_general(q_low, z_high, dims, preferred_element_type=F32)
        x = x_ref[part, lanes] - (both[:, :half] + (both[:, half:] + rest))
        sol[part, :] = jnp.where(live, x, 0.0)


def factor_kernel(dims, count_ref, low_own, low_other, k_own, k_other, h_ref, x_own, x_other, w_ref, *refs):
    wide, scale, parts = dims
    sol_out, left_out, right_out, left, right, sems = refs
    sender = Sender(sems)
    half = x_own.shape[1]
    sender.send(x_own, sol_out.at[:, half_lanes(True, half)])
    sender.send(x_other, sol_out.at[:, half_lanes(False, half)])
    rank = k_own.shape[0]
    low = wide - rank
    at = wide + 2 * low
    (block,) = unpack(h_ref, 0, 1, rank)
    l_top = whole(low_own, low_other, at, rank) - dot(block, whole(low_own, low_other, at + rank, rank))
    l = jnp.concatenate([whole(low_own, low_other, wide, low), l_top * scale], 0)
    k_low = jnp.concatenate([low_own[wide + low : at, :], low_other[wide + low : at, :]], 1)
    k = jnp.concatenate([k_low, jnp.concatenate([k_own[...], k_other[...]], 1) * scale], 0)
    for first, size in parts:
        part, place = slice(first, first + size), pl.ds(first, size)
        live = first + lax.broadcasted_iota(jnp.int32, (1, size), 1) < count_ref[:1, :1]
        left_now = dot(l, w_ref[part, :], ((1,), (1,)))
        left[:, part] = jnp.where(live, left_now, 0.0).astype(left.dtype)
        sender.send(left.at[:, place], left_out.at[:, place])
        x = jnp.concatenate([x_own[part, :], x_other[part, :]], 1)
        right[:, part] = dot(k, x, ((1,), (1,))).astype(right.dtype)
        sender.send(right.at[:, place], right_out.at[:, place])
    sender.wait()


def swapped(value, bit):
    mask = 2**bit
    pairs = [(source, source ^ mask) for source in range(lax.axis_size("leaf"))]
    return lax.ppermute(value, "leaf", pairs)


def shape(*sizes, dtype=F32):
    return jax.ShapeDtypeStruct(sizes, dtype)


def body(right_side, cotangent, coeff_basis, saved_basis, node_inverse, leaf_rows):
    row_count, col_count = right_side.shape
    levels, rank = coeff_basis.shape[:2]
    wide, order, half = levels * rank, 2 * rank, col_count // 2
    low, top = wide - rank, levels - 1
    base_bits = lax.axis_size("leaf").bit_length() - 1 - levels
    pair = base_bits == 0
    chunk = min(512, row_count)
    steps = row_count // chunk
    parts = row_parts(row_count)
    last_parts = last_row_parts(row_count)
    u_all = coeff_basis.reshape(wide, row_count)
    q_all = saved_basis.reshape(wide, row_count)

    vmem = pl.BlockSpec(memory_space=pltpu.VMEM)
    anywhere = pl.BlockSpec(memory_space=pl.ANY)
    small = pltpu.CompilerParams(vmem_limit_bytes=4 * MIB)
    large = pltpu.CompilerParams(vmem_limit_bytes=20 * MIB)

    def call(kernel, name, out_shape, *operands, out_specs=vmem, scratch=(), params=small, cost=None, **options):
        if isinstance(out_shape, list) and out_specs is vmem:
            out_specs = [vmem] * len(out_shape)
        if cost is not None:
            options["cost_estimate"] = pl.CostEstimate(flops=cost, bytes_accessed=MIB, transcendentals=0)
        return pl.pallas_call(
            kernel,
            out_shape=out_shape,
            in_specs=[vmem] * len(operands),
            out_specs=out_specs,
            scratch_shapes=list(scratch),
            compiler_params=params,
            name=name,
            **options,
        )(*operands)

    n_solve = sum(solve_rows(k, levels, rank) for k in range(levels))
    n_side = [side_rows(k, levels, rank) for k in range(levels)]
    arrays = (right_side, cotangent, u_all, q_all)
    outs = [shape(n_solve, half), shape(n_solve, half), shape(wide, wide), shape(levels, order, order)]
    outs += [shape(*a.shape) for a in arrays]
    count = jnp.broadcast_to(leaf_rows[:, None], (8, 128))
    hbm = [pltpu.with_memory_space_constraint(a, pltpu.HBM) for a in (*arrays, node_inverse)]
    solve, solve_send, products, nodes, x_vmem, w_vmem, u_vmem, q_vmem = pl.pallas_call(
        functools.partial(local_kernel, (levels, rank, base_bits), parts, min(3, len(parts))),
        out_shape=outs,
        in_specs=[vmem] + [anywhere] * 5,
        out_specs=[vmem] * 8,
        scratch_shapes=[
            pltpu.VMEM((wide, col_count), F32),
            pltpu.SemaphoreType.DMA((len(parts), 3)),
            pltpu.SemaphoreType.DMA,
            pltpu.SemaphoreType.DMA((levels,)),
        ],
        compiler_params=large,
        name="local_sums",
    )(count, *hbm)
    k_sums = call(
        side_kernel,
        "side_sums",
        shape(wide, col_count),
        count,
        w_vmem,
        u_vmem,
        params=large,
        cost=6 * wide * row_count * col_count,
    )

    def lowest(solve, solve_send):
        if pair:
            return solve, swapped(solve_send, 0)
        solve = solve + swapped(solve_send, 0)
        for bit in range(1, base_bits):
            solve = solve + swapped(solve, bit)
        return solve, swapped(solve, base_bits)

    solve, sib_solve = lowest(solve, solve_send)
    own_solve = solve
    solves, zs, fresh = [], [], {}
    for k in range(levels):
        if k > 0:
            sib_solve = swapped(solve, base_bits + k)
        solves.append(sib_solve)
        placed = []
        if k == 1:
            top_got = swapped(fresh[top], base_bits + top)
            sent = fresh[top - 1]
            got = swapped(sent, base_bits + top - 1)
        elif 1 < k < top:
            bit = top - k
            sent = call(
                functools.partial(side_join_kernel, n_side[bit + 1]),
                f"side_join_{bit}",
                shape(sum(n_side[bit:]), half),
                fresh[bit],
                sent,
                got,
                zs[-1],
                *([top_got] if k == 2 else []),
                cost=2 * 10**10,
            )
            got = swapped(sent, base_bits + bit)
            placed = [sent]
        elif k == top:
            top_sum = call(side_top_kernel, "side_top", shape(n_side[top], half), sent, got, zs[-1])
            top_got = swapped(top_sum, base_bits + top - 1)
            placed = [top_sum]
        out_shape = [shape(order, half)]
        if k < top:
            out_shape.append(shape(sum(solve_rows(i, levels, rank) for i in range(k + 1, levels)), half))
        outs = call(
            functools.partial(level_kernel, (levels, rank, base_bits, len(placed)), k),
            f"level_{k}",
            out_shape,
            solve,
            sib_solve,
            nodes,
            *placed,
            cost=2 * 10**10,
        )
        zs.append(outs[0])
        if k < top:
            solve = outs[1]
        if k == 0:
            side, side_send = call(
                functools.partial(side_state_kernel, (levels, rank)),
                "side_state",
                [shape(sum(n_side), half)] * 2,
                k_sums,
                products,
                outs[0],
            )
            side, sib_side = lowest(side, side_send)
            first = call(
                functools.partial(side_first_kernel, n_side[0]),
                "side_first",
                [shape(size, half) for size in n_side[1:]],
                side,
                sib_side,
                outs[0],
            )
            fresh = dict(enumerate(first, 1))

    dims = (levels, rank, 1.0 / col_count**0.5)
    copies = 2 if pair else 1
    *low_other, low_own = call(
        functools.partial(end_low_kernel, dims, pair),
        "end_low",
        [shape(wide + 2 * low + order, half)] * copies,
        *solves,
        *zs,
        sib_side,
        sent,
        got,
        own_solve,
        side,
        scratch=[pltpu.VMEM((sum(n_side[1:top]), half), F32)],
    )
    low_other = swapped(low_other[0] if pair else low_own, 0)
    k_own, h_top = call(
        end_top_kernel,
        "end_top",
        [shape(rank, half), shape(n_side[top] - rank, half)],
        top_sum,
        top_got,
        cost=2 * 10**10,
    )
    k_other = swapped(k_own, 0)

    sol_own = call(
        functools.partial(solution_kernel, (True, rank, chunk)),
        "solution_own",
        shape(row_count, half),
        count,
        x_vmem,
        q_vmem,
        *zs,
        params=large,
        cost=10**9,
    )
    sol_other = call(
        functools.partial(solution_kernel, (False, rank, chunk)),
        "solution_other",
        shape(row_count, half),
        count,
        x_vmem,
        q_vmem,
        low_other,
        params=large,
        cost=10**9,
    )
    grad = shape(wide, row_count, dtype=jnp.bfloat16)
    sol, left, right = call(
        functools.partial(factor_kernel, (wide, dims[2], last_parts)),
        "factor_rows",
        [shape(row_count, col_count), grad, grad],
        count,
        low_own,
        low_other,
        k_own,
        k_other,
        h_top,
        sol_own,
        sol_other,
        w_vmem,
        out_specs=[anywhere] * 3,
        scratch=[pltpu.VMEM(grad.shape, grad.dtype)] * 2 + [pltpu.SemaphoreType.DMA((2 * len(last_parts) + 2,))],
        params=large,
    )
    return sol, left.reshape(coeff_basis.shape), right.reshape(coeff_basis.shape)


def solution(mesh):
    in_specs = (
        P(("groups", "leaf"), None),
        P(("groups", "leaf"), None),
        P(None, None, ("groups", "leaf")),
        P(None, None, ("groups", "leaf")),
        P("groups", None, None),
        P(("groups", "leaf")),
    )
    out_specs = (
        P(("groups", "leaf"), None),
        P(None, None, ("groups", "leaf")),
        P(None, None, ("groups", "leaf")),
    )
    return jax.shard_map(body, mesh=mesh, in_specs=in_specs, out_specs=out_specs, check_vma=False)
```
